512 devices in a mesh: gx: 8 (over x, core), gy: 8 (over z), gz: 8 (over y).
Axes of the slice: x: 4, y: 8, z: 8, core: 2. Of those that a mesh axis runs over, the one named last changes fastest.
Arguments:
- velocity: float32 [3, 128, 128, 1024], P(None, 'gx', 'gy', 'gz'), may hold values from -6 to 6
- input_weight: bfloat16 [32, 9], replicated, may hold values from -2 to 2
- input_bias: float32 [32], replicated, may hold values from -3 to 3
- hidden_weight: bfloat16 [32, 32], replicated, may hold values from -1 to 1
- hidden_bias: float32 [32], replicated, may hold values from -3 to 3
- output_weight: bfloat16 [32], replicated, may hold values from -1 to 1
Outputs:
- velocity_new: float32 [3, 128, 128, 1024], P(None, 'gx', 'gy', 'gz')
- pressure: float32 [128, 128, 1024], P('gx', 'gy', 'gz')
The draws below stay inside these ranges and needn't reach their ends.
All inputs are finite; a program needn't handle non-finite values.
Results may differ from the reference program's by a relative error of at most 0.00039.
Values sent between devices are 32-bit elements; how exact they have to be, the bound alone decides.
A program may use at most 64 MiB of HBM per device.

```python
import jax
import jax.numpy as jnp
from jax import lax

HID = 32
FEAT = 9
LEVELS = 4
NX = 128
NY = 128
NZ = 1024


def shard_levels(key, extent, pieces, low, top_value):
    factor_of = 1.0
    for position, shards_of in pieces:
        steps = jax.random.uniform(jax.random.fold_in(jax.random.fold_in(key, 6), position), (shards_of,), jnp.float32, low / len(pieces), top_value / len(pieces))
        factor_of = factor_of * jnp.repeat(jnp.exp(steps), extent[position] // shards_of).reshape((-1,) + (1,) * (len(extent) - 1 - position))
    return factor_of


def noise(stream_key, shape, scale, bound, shards=(), dtype=jnp.bfloat16):
    array = jax.random.normal(stream_key, shape, jnp.float32) * scale
    if len(shards) > 0:
        array = shard_levels(stream_key, shape, shards, -0.22, 0.18) * array
    return jnp.clip(array, min=-bound, max=bound).astype(dtype)


def setup_inputs(seed: int = 0) -> dict:
    key_list = jax.random.split(jax.random.key(seed), 7)
    return {
        "velocity": noise(key_list[0], (3, NX, NY, NZ), 1.0, 6.0, ((1, 8), (2, 8), (3, 8)), jnp.float32),
        "input_weight": noise(key_list[1], (HID, FEAT), FEAT ** -0.5, 2.0),
        "input_bias": noise(key_list[2], (HID,), 0.5, 3.0, (), jnp.float32),
        "hidden_weight": noise(key_list[3], (HID, HID), HID ** -0.5, 1.0),
        "hidden_bias": noise(key_list[4], (HID,), 0.5, 3.0, (), jnp.float32),
        "output_weight": noise(key_list[5], (HID,), HID ** -0.5, 1.0),
    }


time_step = 0.1
closure_gain = 0.5
jacobi_weight = 0.8


def forward_of(field, direction):
    return jnp.roll(field, -1, direction)


def backward_of(field, direction):
    return jnp.roll(field, 1, direction)


def laplace(field, grid_level):
    summed = forward_of(field, 0) + backward_of(field, 0)
    summed = summed + forward_of(field, 1) + backward_of(field, 1)
    summed = summed + forward_of(field, 2) + backward_of(field, 2)
    return (summed - 6.0 * field) * (0.25 ** grid_level)


def restrict(fine):
    shaped = fine.reshape(fine.shape[0] // 2, 2, fine.shape[1] // 2, 2, fine.shape[2] // 2, 2)
    return 0.125 * shaped.sum(axis=(1, 3, 5))


def prolong(coarse):
    return jnp.repeat(jnp.repeat(jnp.repeat(coarse, 2, 0), 2, 1), 2, 2)


def multigrid_cycle(source, grid_level):
    factor = jacobi_weight * 4.0 ** grid_level / 6.0
    iterate = jnp.zeros_like(source)
    iterate = iterate - factor * (source - laplace(iterate, grid_level))
    iterate = iterate - factor * (source - laplace(iterate, grid_level))
    if grid_level < LEVELS - 1:
        residual = source - laplace(iterate, grid_level)
        iterate = iterate + prolong(multigrid_cycle(restrict(residual), grid_level + 1))
    for sweep_count in range(2):
        iterate = iterate - factor * (source - laplace(iterate, grid_level))
    return iterate


def reference(velocity, input_weight, input_bias, hidden_weight, hidden_bias, output_weight):
    gradient = [[0.5 * (forward_of(velocity[component], direction) - backward_of(velocity[component], direction))
                 for direction in range(3)] for component in range(3)]
    listing = [gradient[0][0], gradient[1][1], gradient[2][2],
               0.5 * (gradient[0][1] + gradient[1][0]), 0.5 * (gradient[0][2] + gradient[2][0]),
               0.5 * (gradient[1][2] + gradient[2][1]),
               0.5 * (gradient[0][1] - gradient[1][0]), 0.5 * (gradient[0][2] - gradient[2][0]),
               0.5 * (gradient[1][2] - gradient[2][1])]
    count_x = velocity.shape[1]
    features = jnp.stack([entry.reshape(count_x, -1) for entry in listing], axis=1).astype(jnp.bfloat16)
    first_weight = input_weight.astype(jnp.float32)
    second_weight = hidden_weight.astype(jnp.float32)
    last_weight = output_weight.astype(jnp.float32)

    def apply_slab(slab_cells):
        hidden = jnp.tanh(jnp.dot(first_weight, slab_cells.astype(jnp.float32), precision=lax.Precision.HIGHEST)
                          + input_bias[:, None]).astype(jnp.bfloat16)
        second = jnp.tanh(jnp.dot(second_weight, hidden.astype(jnp.float32), precision=lax.Precision.HIGHEST)
                          + hidden_bias[:, None]).astype(jnp.bfloat16)
        return closure_gain * jax.nn.softplus(jnp.dot(last_weight, second.astype(jnp.float32), precision=lax.Precision.HIGHEST))

    viscosity = lax.map(apply_slab, features).reshape(velocity.shape[1:])
    provisional_list = []
    for component in range(3):
        advect = 0.0
        diffuse = 0.0
        for direction in range(3):
            product = velocity[direction] * velocity[component]
            advect = advect + 0.5 * (forward_of(product, direction) - backward_of(product, direction))
            upward = 0.5 * (viscosity + forward_of(viscosity, direction)) * (forward_of(velocity[component], direction) - velocity[component])
            downward = 0.5 * (viscosity + backward_of(viscosity, direction)) * (velocity[component] - backward_of(velocity[component], direction))
            diffuse = diffuse + (upward - downward)
        provisional_list.append(velocity[component] + time_step * (diffuse - advect))
    provisional = jnp.stack(provisional_list)
    divergence = 0.0
    for direction in range(3):
        divergence = divergence + 0.5 * (forward_of(provisional[direction], direction) - backward_of(provisional[direction], direction))
    pressure = multigrid_cycle(divergence, 0)
    velocity_new = jnp.stack([provisional[direction] - 0.5 * (forward_of(pressure, direction) - backward_of(pressure, direction))
                              for direction in range(3)])
    return velocity_new, pressure
```

```python
import jax
import jax.numpy as jnp
from jax import lax
from jax.experimental import pallas as pl
from jax.experimental.pallas import tpu as pltpu
from jax.sharding import PartitionSpec as P

MESH = pl.DeviceIdType.MESH
AXES = ("gx", "gy", "gz")
F32, BF16 = jnp.float32, jnp.bfloat16
EXACT = lax.Precision.HIGHEST

TIME_STEP = 0.1
GAIN = 0.5
C = 0.8 / 6.0

FACES = [(1, 0, 0), (-1, 0, 0), (0, 1, 0), (0, -1, 0), (0, 0, 1), (0, 0, -1)]
AROUND = [
    (i, j, k) for i in (-1, 0, 1) for j in (-1, 0, 1) for k in (-1, 0, 1) if (i, j, k) != (0, 0, 0)
]
PLANE_ROWS = 24
N_COPIES = 6 * 3 + 26 * 2 + 20 + 6


def lanes(shape):
    return lax.broadcasted_iota(jnp.int32, shape, len(shape) - 1)


def rows_of(shape):
    return lax.broadcasted_iota(jnp.int32, shape, len(shape) - 2)


def lane_roll(value, shift):
    return pltpu.roll(value, shift % 128, value.ndim - 1)


def dot(a, b, precision=None):
    return jnp.dot(a, b, precision=precision, preferred_element_type=F32)


def coarse_lane(shape, axis):
    fine = lax.broadcasted_iota(jnp.int32, shape, axis)
    return jnp.where(fine < 192, 32 + fine // 2, fine // 2 - 96)


class Copies:
    def __init__(self, ids, send_sem, recv_sem):
        self.ids, self.send_sem, self.recv_sem = ids, send_sem, recv_sem
        self.made = []

    def device(self, offset):
        return tuple(lax.rem(i + 8 + o, 8) for i, o in zip(self.ids, offset))

    def start(self, src, dst, offset):
        k = len(self.made)
        copy = pltpu.make_async_remote_copy(
            src_ref=src,
            dst_ref=dst,
            send_sem=self.send_sem.at[k],
            recv_sem=self.recv_sem.at[k],
            device_id=self.device(offset),
            device_id_type=MESH,
        )
        copy.start()
        self.made.append(copy)
        return copy


def sum6(ref, base, n, period):
    center = ref[pl.ds(base, n), :]
    total = ref[pl.ds(base + period, n), :] + ref[pl.ds(base - period, n), :]
    total = total + ref[pl.ds(base + 1, n), :] + ref[pl.ds(base - 1, n), :]
    return center, total + lane_roll(center, 1) + lane_roll(center, -1)


def sum6_wide(ref, base, n, period):
    center = [ref[t, pl.ds(base, n), :] for t in (0, 1)]
    lane = lanes((n, 128))
    up = [lane_roll(c, -1) for c in center]
    down = [lane_roll(c, 1) for c in center]
    out = []
    for t in (0, 1):
        total = ref[t, pl.ds(base + period, n), :] + ref[t, pl.ds(base - period, n), :]
        total = total + ref[t, pl.ds(base + 1, n), :] + ref[t, pl.ds(base - 1, n), :]
        total = total + jnp.where(lane == 127, up[1 - t], up[t])
        out.append(total + jnp.where(lane == 0, down[1 - t], down[t]))
    return center, out


def kernel(
    vel, w1, b1, w2, b2, w3, vout, pout,
    w1k, w2k, w3k, b1k, b2k,
    vb, nb, pb, sy, sz, rz,
    dv, sdz, rdx, rdy, rde, rdz, db, v0, u0,
    rs, rt, s1, v1s, r1c, sez, rex, rey, ree, rez, lb1, v1, u1,
    sa, ra, sb, rb, lb2, v2, u2, lb3, v3, u3,
    send_sem, recv_sem,
):
    ids = [lax.axis_index(a) for a in AXES]
    cp = Copies(ids, send_sem, recv_sem)
    barrier = pltpu.get_barrier_semaphore()
    for offset in FACES:
        pl.semaphore_signal(barrier, inc=1, device_id=cp.device(offset), device_id_type=MESH)

    def place(p, carry):
        base = pl.multiple_of(8 + PLANE_ROWS * (p + 1), 8)
        for c in range(3):
            vb[c, pl.ds(base, 16), :] = vel[c, p]
        return carry

    lax.fori_loop(0, 16, place, 0, unroll=True)

    def pack_faces(ref2d, which):
        lane = lanes((16, 128))
        packed = jnp.zeros((16, 128), F32)
        for c, load in enumerate(ref2d):
            sy[which, 0, c] = load(pl.ds(8 + PLANE_ROWS, 16, stride=PLANE_ROWS))
            sy[which, 1, c] = load(pl.ds(8 + PLANE_ROWS + 15, 16, stride=PLANE_ROWS))
            for x in range(16):
                plane = load(pl.ds(8 + PLANE_ROWS * (x + 1), 16))
                packed = jnp.where(lane // 2 == 4 * x + c, lane_roll(plane, 8 * x + 2 * c + 1), packed)
        sz[which] = packed

    pack_faces([lambda d, c=c: vb[c, d, :] for c in range(3)], 0)

    pl.semaphore_wait(barrier, len(FACES))

    low, high = 8, 8 + PLANE_ROWS * 17
    first, last = 8 + PLANE_ROWS, 8 + PLANE_ROWS * 16
    vel_copies = [
        cp.start(vel.at[:, 0], vb.at[:, pl.ds(high, 16), :], (-1, 0, 0)),
        cp.start(vel.at[:, 15], vb.at[:, pl.ds(low, 16), :], (1, 0, 0)),
        cp.start(sy.at[0, 0], rz.at[0, 1], (0, -1, 0)),
        cp.start(sy.at[0, 1], rz.at[0, 0], (0, 1, 0)),
        cp.start(sz.at[0], rz.at[0, 2, 1], (0, 0, -1)),
        cp.start(sz.at[0], rz.at[0, 2, 0], (0, 0, 1)),
    ]

    spread = (rows_of((256, 32)) // 8 == lanes((256, 32))).astype(BF16)
    spread_t = (rows_of((32, 256)) == lanes((32, 256)) // 8).astype(BF16)
    columns = (rows_of((9, 80)) == lanes((9, 80)) // 8).astype(BF16)
    wide = dot(dot(spread, w1[...]).astype(BF16), columns)
    same = rows_of((256, 80)) % 8 == lanes((256, 80)) % 8
    w1k[...] = jnp.where(same, wide, 0.0).astype(BF16)
    wide = dot(dot(spread, w2[...]).astype(BF16), spread_t)
    same = rows_of((256, 256)) % 8 == lanes((256, 256)) % 8
    w2k[...] = jnp.where(same, wide, 0.0).astype(BF16)
    wide = jnp.broadcast_to(dot(w3[...], spread_t), (16, 256))
    same = rows_of((16, 256)) == lanes((16, 256)) % 8
    w3k[...] = jnp.where(same, wide, 0.0).astype(BF16)
    mine = rows_of((256, 32)) // 8 == lanes((256, 32))
    for bias, kept in ((b1, b1k), (b2, b2k)):
        column = jnp.sum(jnp.where(mine, bias[...], 0.0), axis=1, keepdims=True)
        kept[...] = jnp.broadcast_to(column, (256, 128))
    lb2[...] = jnp.zeros_like(lb2)

    for c in vel_copies:
        c.wait_recv()
    for c in range(3):
        vb[c, pl.ds(8 + PLANE_ROWS - 1, 16, stride=PLANE_ROWS), :] = rz[0, 0, c]
        vb[c, pl.ds(8 + PLANE_ROWS + 16, 16, stride=PLANE_ROWS), :] = rz[0, 1, c]

    lane16 = lanes((16, 128))

    def z_next(plane, halo, x, c):
        beyond = pltpu.roll(halo, lax.rem(254 - 8 * x - 2 * c, 128), 1)
        return jnp.where(lane16 == 127, beyond, lane_roll(plane, -1))

    def z_last(plane, halo, x, c):
        beyond = pltpu.roll(halo, lax.rem(256 - 8 * x - 2 * c, 128), 1)
        return jnp.where(lane16 == 0, beyond, lane_roll(plane, 1))

    def neighbours(load, x, base, which, c):
        plane = load(base)
        return plane, [
            (load(base + PLANE_ROWS), load(base - PLANE_ROWS)),
            (load(base + 1), load(base - 1)),
            (z_next(plane, rz[which, 2, 1], x, c), z_last(plane, rz[which, 2, 0], x, c)),
        ]

    def vel_load(c):
        return lambda base: vb[c, pl.ds(base, 16), :]

    def closure(x, carry):
        base = pl.multiple_of(8 + PLANE_ROWS * (x + 1), 8)
        g = []
        for c in range(3):
            _, around = neighbours(vel_load(c), x, base, 0, c)
            g.append([0.5 * (a - b) for a, b in around])
        listing = [
            g[0][0], g[1][1], g[2][2],
            0.5 * (g[0][1] + g[1][0]), 0.5 * (g[0][2] + g[2][0]), 0.5 * (g[1][2] + g[2][1]),
            0.5 * (g[0][1] - g[1][0]), 0.5 * (g[0][2] - g[2][0]), 0.5 * (g[1][2] - g[2][1]),
        ]
        listing.append(jnp.zeros((16, 128), F32))
        features = jnp.concatenate(
            [jnp.concatenate([entry[0:8], entry[8:16]], axis=1) for entry in listing], axis=0
        ).astype(BF16)
        bias = jnp.concatenate([b1k[...]] * 2, axis=1)
        hidden = jnp.tanh(dot(w1k[...], features) + bias).astype(BF16)
        bias = jnp.concatenate([b2k[...]] * 2, axis=1)
        second = jnp.tanh(dot(w2k[...], hidden) + bias).astype(BF16)
        s = dot(w3k[...], second)[0:8]
        soft = GAIN * (jnp.maximum(s, 0.0) + jnp.log1p(jnp.exp(-jnp.abs(s))))
        nb[pl.ds(base, 16), :] = jnp.concatenate([soft[:, 0:128], soft[:, 128:256]], axis=0)
        return carry

    lax.fori_loop(0, 16, closure, 0)

    pack_faces([lambda d: nb[d, :]], 1)
    visc_copies = [
        cp.start(nb.at[pl.ds(first, 16), :], nb.at[pl.ds(high, 16), :], (-1, 0, 0)),
        cp.start(nb.at[pl.ds(last, 16), :], nb.at[pl.ds(low, 16), :], (1, 0, 0)),
        cp.start(sy.at[1, 0, 0], rz.at[1, 1, 0], (0, -1, 0)),
        cp.start(sy.at[1, 1, 0], rz.at[1, 0, 0], (0, 1, 0)),
        cp.start(sz.at[1], rz.at[1, 2, 1], (0, 0, -1)),
        cp.start(sz.at[1], rz.at[1, 2, 0], (0, 0, 1)),
    ]
    for c in visc_copies:
        c.wait_recv()
    nb[pl.ds(8 + PLANE_ROWS - 1, 16, stride=PLANE_ROWS), :] = rz[1, 0, 0]
    nb[pl.ds(8 + PLANE_ROWS + 16, 16, stride=PLANE_ROWS), :] = rz[1, 1, 0]

    def tendency(x, carry):
        base = pl.multiple_of(8 + PLANE_ROWS * (x + 1), 8)
        mid, thick = neighbours(lambda r: nb[pl.ds(r, 16), :], x, base, 1, 0)
        thick = [(0.5 * (mid + a), 0.5 * (mid + b)) for a, b in thick]
        all_v = [neighbours(vel_load(c), x, base, 0, c) for c in range(3)]
        for i in range(3):
            center, around = all_v[i]
            change = 0.0
            for j in range(3):
                (up, down), (up_j, down_j) = around[j], all_v[j][1][j]
                change = change + thick[j][0] * (up - center) - thick[j][1] * (center - down)
                change = change - 0.5 * (up_j * up - down_j * down)
            pb[i, pl.ds(base, 16), :] = center + TIME_STEP * change
        return carry

    lax.fori_loop(0, 16, tendency, 0, unroll=2)

    sy[2, 0, 0] = pb[1, pl.ds(first, 16, stride=PLANE_ROWS), :]
    sy[2, 1, 0] = pb[1, pl.ds(first + 15, 16, stride=PLANE_ROWS), :]
    packed = jnp.zeros((16, 128), F32)
    for x in range(16):
        plane = pb[2, pl.ds(8 + PLANE_ROWS * (x + 1), 16), :]
        packed = jnp.where(lane16 // 2 == 4 * x, lane_roll(plane, 8 * x + 1), packed)
    sz[2] = packed
    prov_copies = [
        cp.start(pb.at[0, pl.ds(first, 16), :], pb.at[0, pl.ds(high, 16), :], (-1, 0, 0)),
        cp.start(pb.at[0, pl.ds(last, 16), :], pb.at[0, pl.ds(low, 16), :], (1, 0, 0)),
        cp.start(sy.at[2, 0, 0], rz.at[2, 1, 0], (0, -1, 0)),
        cp.start(sy.at[2, 1, 0], rz.at[2, 0, 0], (0, 1, 0)),
        cp.start(sz.at[2], rz.at[2, 2, 1], (0, 0, -1)),
        cp.start(sz.at[2], rz.at[2, 2, 0], (0, 0, 1)),
    ]
    for c in prov_copies:
        c.wait_recv()
    pb[1, pl.ds(first - 1, 16, stride=PLANE_ROWS), :] = rz[2, 0, 0]
    pb[1, pl.ds(first + 16, 16, stride=PLANE_ROWS), :] = rz[2, 1, 0]

    for x in range(16):
        base = 8 + PLANE_ROWS * (x + 1)
        plane = pb[2, pl.ds(base, 16), :]
        total = pb[0, pl.ds(base + PLANE_ROWS, 16), :] - pb[0, pl.ds(base - PLANE_ROWS, 16), :]
        total = total + pb[1, pl.ds(base + 1, 16), :] - pb[1, pl.ds(base - 1, 16), :]
        beyond = jnp.where(lane16 == 127, lane_roll(rz[2, 2, 1], 126 - 8 * x), lane_roll(plane, -1))
        before = jnp.where(lane16 == 0, lane_roll(rz[2, 2, 0], -8 * x), lane_roll(plane, 1))
        dv[x] = 0.5 * (total + (beyond - before))

    for half in range(2):
        packed = jnp.zeros((16, 128), F32)
        for k in range(8):
            packed = jnp.where(lane16 // 16 == k, lane_roll(dv[8 * half + k], 16 * k + 8), packed)
        sdz[half] = packed
    div_copies = []
    for dx, dy, dz in AROUND:
        here_x, here_y = (1 - dx) // 2, (1 - dy) // 2
        if dz == 0:
            if dy == 0:
                src, dst = dv.at[pl.ds(10 if dx > 0 else 0, 6)], rdx.at[here_x]
            elif dx == 0:
                src, dst = dv.at[:, pl.ds(8 if dy > 0 else 0, 8), :], rdy.at[here_y]
            else:
                src = dv.at[pl.ds(10 if dx > 0 else 0, 6), pl.ds(8 if dy > 0 else 0, 8), :]
                dst = rde.at[here_x, here_y]
        else:
            half = pl.ds(0, 2) if dx == 0 else pl.ds(1 if dx > 0 else 0, 1)
            slot = pl.ds(1, 2) if dx == 0 else pl.ds(0 if dx > 0 else 3, 1)
            part = pl.ds(0, 16) if dy == 0 else pl.ds(8 if dy > 0 else 0, 8)
            rows = pl.ds(8, 16) if dy == 0 else pl.ds(0 if dy > 0 else 24, 8)
            src, dst = sdz.at[half, part, :], rdz.at[(1 - dz) // 2, slot, rows, :]
        div_copies.append(cp.start(src, dst, (dx, dy, dz)))

    def at0(p):
        return 8 + 32 * p

    for x in range(16):
        db[0, pl.ds(at0(x + 6) + 8, 16), :] = dv[x]
    for c in div_copies:
        c.wait_recv()
    for x in range(6):
        for side, p in ((0, x), (1, 22 + x)):
            db[0, pl.ds(at0(p) + 8, 16), :] = rdx[side, x]
            db[0, pl.ds(at0(p), 8), :] = rde[side, 0, x]
            db[0, pl.ds(at0(p) + 24, 8), :] = rde[side, 1, x]
    for x in range(16):
        db[0, pl.ds(at0(x + 6), 8), :] = rdy[0, x]
        db[0, pl.ds(at0(x + 6) + 24, 8), :] = rdy[1, x]
    lane32 = lanes((32, 128))
    for g in range(4):
        both = jnp.where(lane32 % 16 < 8, rdz[0, g], rdz[1, g])
        for k in range(8):
            x = 8 * (g - 1) + k
            if -6 <= x < 22:
                db[1, pl.ds(at0(x + 6), 32), :] = lane_roll(both, -(16 * k + 8))

    for p in range(1, 27, 2):
        b, around = sum6_wide(db, at0(p), 64, 32)
        for t in (0, 1):
            v0[t, pl.ds(at0(p), 64), :] = -C * (1.2 * b[t] + C * around[t])
    for k in range(12):
        base = at0(2 + 2 * k)
        v, around = sum6_wide(v0, base, 64, 32)
        for t in (0, 1):
            residual = db[t, pl.ds(base, 64), :] - (around[t] - 6.0 * v[t])
            rs[pl.ds(32 * k, 32), pl.ds(128 * t, 128)] = residual[0:32] + residual[32:64]
    halve = jnp.where(coarse_lane((256, 128), 0) == lanes((256, 128)), 0.125, 0.0).astype(F32)
    rt[...] = dot(rs[...], halve, EXACT)
    s1[...] = rt[pl.ds(0, 192, stride=2), :] + rt[pl.ds(1, 192, stride=2), :]

    lane8 = lanes((8, 128))
    packed = jnp.zeros((8, 128), F32)
    for x in range(8):
        plane = s1[pl.ds(16 * (x + 2) + 4, 8), :]
        r1c[x] = plane
        packed = jnp.where(lane8 // 8 == 2 * x, lane_roll(plane, 16 * x - 88), packed)
        packed = jnp.where(lane8 // 8 == 2 * x + 1, lane_roll(plane, 16 * x + 8 - 32), packed)
    sez[...] = packed

    for p in range(1, 11, 5):
        b, around = sum6(s1, 16 * p, 80, 16)
        v1s[pl.ds(16 * p, 80), :] = -4.0 * C * (1.2 * b + C * around)
    parts = []
    for k in range(4):
        base = 16 * (2 + 2 * k)
        v, around = sum6(v1s, base, 32, 16)
        residual = s1[pl.ds(base, 32), :] - 0.25 * (around - 6.0 * v)
        parts.append(residual[0:16] + residual[16:32])
    halve = halve[0:128]
    rt[pl.ds(0, 64), :] = dot(jnp.concatenate(parts, axis=0), halve, EXACT)
    packed = jnp.zeros((8, 128), F32)
    for x in range(4):
        plane = rt[pl.ds(16 * x, 8, stride=2), :] + rt[pl.ds(16 * x + 1, 8, stride=2), :]
        packed = jnp.where(lane8 // 32 == x, lane_roll(plane, 32 * x - 48), packed)
    sa[...] = packed
    ra[3, 1] = packed
    xz_copies = [
        cp.start(sa, ra.at[3 - dx, 1 - dz], (dx, 0, dz))
        for dx in range(-3, 4)
        for dz in (-1, 0, 1)
        if (dx, dz) != (0, 0)
    ]
    src_copies = []
    for dx, dy, dz in AROUND:
        here_x, here_y = (1 - dx) // 2, (1 - dy) // 2
        if dz == 0:
            planes = pl.ds(3 if dx > 0 else 0, 5)
            if dy == 0:
                src, dst = r1c.at[planes], rex.at[here_x]
            elif dx == 0:
                src, dst = r1c, rey.at[here_y]
            else:
                src, dst = r1c.at[planes], ree.at[here_x, here_y]
        else:
            src, dst = sez, rez.at[(1 - dz) // 2, 1 - dx, pl.ds(8 * (1 - dy), 8), :]
        src_copies.append(cp.start(src, dst, (dx, dy, dz)))

    for c in xz_copies:
        c.wait_recv()
    row8 = rows_of((8, 128))
    kept_rows = (row8 >= 2) & (row8 < 6)
    for dx in range(7):
        four = []
        for x in range(4):
            before, here, after = (
                lane_roll(ra[dx, k], lane - 32 * x) for k, lane in ((0, 16), (1, 48), (2, 80))
            )
            whole = jnp.where(lane8 < 48, before, jnp.where(lane8 < 80, here, after))
            lb2[pl.ds(32 * (4 * dx + x) + 12, 4), :] = whole[2:6]
            four.append(whole)
        pairs = [
            jnp.where(lane8 < 64, lane_roll(four[i], -32), lane_roll(four[i + 1], 32)) for i in (0, 2)
        ]
        sb[dx] = jnp.where(kept_rows, pairs[0], pltpu.roll(pairs[1], 4, 0))
    y_copies = []
    for dy in (1, -1, 2, -2, 3, -3):
        wanted = pl.ds(abs(dy) - 1, 9 - 2 * abs(dy))
        y_copies.append(cp.start(sb.at[wanted], rb.at[3 - dy, wanted], (0, dy, 0)))

    for c in src_copies:
        c.wait_recv()
    lane24 = lanes((24, 128))
    for p in range(18):
        dx, x = (p - 5) // 8, (p - 5) % 8
        if dx == 0:
            three = [rey[0, x], r1c[x], rey[1, x]]
        else:
            side = (dx + 1) // 2
            k = x - 3 if dx < 0 else x
            three = [ree[side, 0, k], rex[side, k], ree[side, 1, k]]
        before = lane_roll(rez[0, dx + 1], 24 - 16 * x)
        after = lane_roll(rez[1, dx + 1], 96 - 16 * x - 8)
        here = jnp.concatenate(three, axis=0)
        lb1[pl.ds(24 * p, 24), :] = jnp.where(
            lane24 < 32, before, jnp.where(lane24 < 96, here, after)
        )
    for p in range(1, 17, 4):
        b, around = sum6(lb1, 24 * p, 96, 24)
        v1[pl.ds(24 * p, 96), :] = -4.0 * C * (1.2 * b + C * around)

    for c in y_copies:
        c.wait_recv()
    for dy in (-3, -2, -1, 1, 2, 3):
        for dx in range(abs(dy) - 1, 8 - abs(dy)):
            tile = rb[3 + dy, dx]
            other = pltpu.roll(tile, 4, 0)
            for x in range(4):
                plane = lane_roll(tile if x < 2 else other, 32 if x % 2 == 0 else -32)
                lb2[pl.ds(32 * (4 * dx + x) + 12 + 4 * dy, 4), :] = plane[2:6]

    for p in range(1, 27, 2):
        b, around = sum6(lb2, 32 * p, 64, 32)
        v2[pl.ds(32 * p, 64), :] = -16.0 * C * (1.2 * b + C * around)
    for k in range(12):
        base = 32 * (2 + 2 * k)
        v, around = sum6(v2, base, 64, 32)
        residual = lb2[pl.ds(base, 64), :] - 0.0625 * (around - 6.0 * v)
        rs[pl.ds(32 * k, 32), pl.ds(0, 128)] = residual[0:32] + residual[32:64]
    rt[...] = dot(rs[:, 0:128], halve, EXACT)
    lb3[...] = rt[pl.ds(0, 192, stride=2), :] + rt[pl.ds(1, 192, stride=2), :]

    b, around = sum6(lb3, 16, 160, 16)
    v3[pl.ds(16, 160), :] = -64.0 * C * (1.2 * b + C * around)
    v, around = sum6(v3, 32, 128, 16)
    u3[pl.ds(32, 128), :] = 0.2 * v + C * around - 64.0 * C * lb3[pl.ds(32, 128), :]
    v, around = sum6(u3, 48, 96, 16)
    coarse = 0.2 * v + C * around - 64.0 * C * lb3[pl.ds(48, 96), :]

    double = jnp.where(rows_of((128, 256)) == coarse_lane((128, 256), 1), 1.0, 0.0).astype(F32)
    fine = dot(coarse, double[:, 0:128], EXACT)
    for k in range(6):
        for p in (8 + 2 * k, 9 + 2 * k):
            for odd in (0, 1):
                where = pl.ds(32 * p + odd, 16, stride=2)
                v2[where, :] = v2[where, :] + fine[16 * k : 16 * k + 16]
    for p in range(9, 19, 2):
        v, around = sum6(v2, 32 * p, 64, 32)
        u2[pl.ds(32 * p, 64), :] = 0.2 * v + C * around - 16.0 * C * lb2[pl.ds(32 * p, 64), :]
    for k in range(4):
        base = 32 * (10 + 2 * k)
        v, around = sum6(u2, base, 64, 32)
        rs[pl.ds(64 * k, 64), pl.ds(0, 128)] = (
            0.2 * v + C * around - 16.0 * C * lb2[pl.ds(base, 64), :]
        )

    fine = dot(rs[0:256, 0:128], double[:, 0:128], EXACT)
    for k in range(8):
        for p in (1 + 2 * k, 2 + 2 * k):
            for odd in (0, 1):
                where = pl.ds(24 * p + odd, 12, stride=2)
                v1[where, :] = v1[where, :] + fine[32 * k + 8 : 32 * k + 20]
    for p in range(2, 16, 2):
        v, around = sum6(v1, 24 * p, 48, 24)
        u1[pl.ds(24 * p, 48), :] = 0.2 * v + C * around - 4.0 * C * lb1[pl.ds(24 * p, 48), :]
    for k in range(6):
        base = 24 * (3 + 2 * k)
        v, around = sum6(u1, base, 48, 24)
        rs[pl.ds(48 * k, 48), pl.ds(0, 128)] = (
            0.2 * v + C * around - 4.0 * C * lb1[pl.ds(base, 48), :]
        )

    for t in (0, 1):
        fine = dot(rs[0:288, 0:128], double[:, 128 * t : 128 * t + 128], EXACT)
        for k in range(12):
            for p in (2 + 2 * k, 3 + 2 * k):
                for odd in (0, 1):
                    where = pl.ds(at0(p) + odd, 16, stride=2)
                    v0[t, where, :] = v0[t, where, :] + fine[24 * k + 4 : 24 * k + 20]
    for p in range(4, 24, 2):
        v, around = sum6_wide(v0, at0(p), 64, 32)
        for t in (0, 1):
            b = db[t, pl.ds(at0(p), 64), :]
            u0[t, pl.ds(at0(p), 64), :] = 0.2 * v[t] + C * around[t] - C * b
    for p in range(5, 23, 2):
        v, around = sum6_wide(u0, at0(p), 64, 32)
        for t in (0, 1):
            b = db[t, pl.ds(at0(p), 64), :]
            v0[t, pl.ds(at0(p), 64), :] = 0.2 * v[t] + C * around[t] - C * b

    for x in range(16):
        base = at0(x + 6) + 8
        here, beyond = v0[0, pl.ds(base, 16), :], v0[1, pl.ds(base, 16), :]
        pout[x] = here
        slopes = [
            v0[0, pl.ds(base + 32, 16), :] - v0[0, pl.ds(base - 32, 16), :],
            v0[0, pl.ds(base + 1, 16), :] - v0[0, pl.ds(base - 1, 16), :],
            jnp.where(lane16 == 127, lane_roll(beyond, -1), lane_roll(here, -1))
            - jnp.where(lane16 == 0, lane_roll(beyond, 1), lane_roll(here, 1)),
        ]
        for c in range(3):
            vout[c, x] = pb[c, pl.ds(8 + PLANE_ROWS * (x + 1), 16), :] - 0.5 * slopes[c]

    for c in cp.made:
        c.wait_send()


def body(velocity, input_weight, input_bias, hidden_weight, hidden_bias, output_weight):
    def scratch(*shape):
        return pltpu.VMEM(shape, F32)

    plane_buffer = 16 + PLANE_ROWS * 18
    level0 = 16 + 32 * 28
    return pl.pallas_call(
        kernel,
        out_shape=(
            jax.ShapeDtypeStruct((3, 16, 16, 128), F32),
            jax.ShapeDtypeStruct((16, 16, 128), F32),
        ),
        in_specs=[pl.BlockSpec(memory_space=pltpu.VMEM)] * 6,
        out_specs=[pl.BlockSpec(memory_space=pltpu.VMEM)] * 2,
        scratch_shapes=[
            pltpu.VMEM((256, 80), BF16),
            pltpu.VMEM((256, 256), BF16),
            pltpu.VMEM((16, 256), BF16),
            scratch(256, 128),
            scratch(256, 128),
            scratch(3, plane_buffer, 128),
            scratch(plane_buffer, 128),
            scratch(3, plane_buffer, 128),
            scratch(3, 2, 3, 16, 128),
            scratch(3, 16, 128),
            scratch(3, 3, 3, 16, 128),
            scratch(16, 16, 128),
            scratch(2, 16, 128),
            scratch(2, 6, 16, 128),
            scratch(2, 16, 8, 128),
            scratch(2, 2, 6, 8, 128),
            scratch(2, 4, 32, 128),
            scratch(2, level0, 128),
            scratch(2, level0, 128),
            scratch(2, level0, 128),
            scratch(384, 256),
            scratch(384, 128),
            scratch(192, 128),
            scratch(192, 128),
            scratch(8, 8, 128),
            scratch(8, 128),
            scratch(2, 5, 8, 128),
            scratch(2, 8, 8, 128),
            scratch(2, 2, 5, 8, 128),
            scratch(2, 3, 24, 128),
            scratch(432, 128),
            scratch(432, 128),
            scratch(432, 128),
            scratch(8, 128),
            scratch(7, 3, 8, 128),
            scratch(7, 8, 128),
            scratch(7, 7, 8, 128),
            scratch(896, 128),
            scratch(896, 128),
            scratch(896, 128),
            scratch(192, 128),
            scratch(192, 128),
            scratch(192, 128),
            pltpu.SemaphoreType.DMA((N_COPIES,)),
            pltpu.SemaphoreType.DMA((N_COPIES,)),
        ],
        compiler_params=pltpu.CompilerParams(
            collective_id=0, has_side_effects=True, vmem_limit_bytes=48 * 1024 * 1024
        ),
    )(
        velocity,
        input_weight,
        input_bias.reshape(1, 32),
        hidden_weight,
        hidden_bias.reshape(1, 32),
        output_weight.reshape(1, 32),
    )


def solution(mesh):
    return jax.shard_map(
        body,
        mesh=mesh,
        in_specs=(P(None, "gx", "gy", "gz"), P(), P(), P(), P(), P()),
        out_specs=(P(None, "gx", "gy", "gz"), P("gx", "gy", "gz")),
        check_vma=False,
    )
```

```python
import jax
import jax.numpy as jnp
from jax import lax
from jax.experimental import pallas as pl
from jax.experimental.pallas import tpu as pltpu
from jax.sharding import PartitionSpec as P

MESH = pl.DeviceIdType.MESH
AXES = ("gx", "gy", "gz")
F32, BF16 = jnp.float32, jnp.bfloat16
EXACT = lax.Precision.HIGHEST

TIME_STEP = 0.1
GAIN = 0.5
C = 0.8 / 6.0

FACES = [(1, 0, 0), (-1, 0, 0), (0, 1, 0), (0, -1, 0), (0, 0, 1), (0, 0, -1)]
AROUND = [
    (i, j, k) for i in (-1, 0, 1) for j in (-1, 0, 1) for k in (-1, 0, 1) if (i, j, k) != (0, 0, 0)
]
PLANE_ROWS = 24
N_COPIES = 6 * 3 + 26 * 2 + 20 + 6


def lanes(shape):
    return lax.broadcasted_iota(jnp.int32, shape, len(shape) - 1)


def rows_of(shape):
    return lax.broadcasted_iota(jnp.int32, shape, len(shape) - 2)


def lane_roll(value, shift):
    return pltpu.roll(value, shift % 128, value.ndim - 1)


def dot(a, b, precision=None):
    return jnp.dot(a, b, precision=precision, preferred_element_type=F32)


def coarse_lane(shape, axis):
    fine = lax.broadcasted_iota(jnp.int32, shape, axis)
    return jnp.where(fine < 192, 32 + fine // 2, fine // 2 - 96)


class Copies:
    def __init__(self, ids, send_sem, recv_sem):
        self.ids, self.send_sem, self.recv_sem = ids, send_sem, recv_sem
        self.made = []

    def device(self, offset):
        return tuple(lax.rem(i + 8 + o, 8) for i, o in zip(self.ids, offset))

    def start(self, src, dst, offset):
        k = len(self.made)
        copy = pltpu.make_async_remote_copy(
            src_ref=src,
            dst_ref=dst,
            send_sem=self.send_sem.at[k],
            recv_sem=self.recv_sem.at[k],
            device_id=self.device(offset),
            device_id_type=MESH,
        )
        copy.start()
        self.made.append(copy)
        return copy


def sum6(ref, base, n, period):
    center = ref[pl.ds(base, n), :]
    total = ref[pl.ds(base + period, n), :] + ref[pl.ds(base - period, n), :]
    total = total + ref[pl.ds(base + 1, n), :] + ref[pl.ds(base - 1, n), :]
    return center, total + lane_roll(center, 1) + lane_roll(center, -1)


def sum6_wide(ref, base, n, period):
    center = [ref[t, pl.ds(base, n), :] for t in (0, 1)]
    lane = lanes((n, 128))
    up = [lane_roll(c, -1) for c in center]
    down = [lane_roll(c, 1) for c in center]
    out = []
    for t in (0, 1):
        total = ref[t, pl.ds(base + period, n), :] + ref[t, pl.ds(base - period, n), :]
        total = total + ref[t, pl.ds(base + 1, n), :] + ref[t, pl.ds(base - 1, n), :]
        total = total + jnp.where(lane == 127, up[1 - t], up[t])
        out.append(total + jnp.where(lane == 0, down[1 - t], down[t]))
    return center, out


def kernel(
    vel_in, w1_in, b1_in, w2_in, b2_in, w3_in, vout, pout,
    vel, w1, b1, w2, b2, w3, w1k, w2k, w3k, b1k, b2k,
    vb, nb, pb, sy, sz, rz,
    dv, sdz, rdx, rdy, rde, rdz, db, v0, u0,
    rs, rt, s1, v1s, r1c, sez, rex, rey, ree, rez, lb1, v1, u1,
    sa, ra, sb, rb, lb2, v2, u2, lb3, v3, u3,
    send_sem, recv_sem, load_sem,
):
    ids = [lax.axis_index(a) for a in AXES]
    cp = Copies(ids, send_sem, recv_sem)
    barrier = pltpu.get_barrier_semaphore()
    for offset in FACES:
        pl.semaphore_signal(barrier, inc=1, device_id=cp.device(offset), device_id_type=MESH)

    loads = [
        pltpu.make_async_copy(src, dst, load_sem.at[k])
        for k, (src, dst) in enumerate(
            ((vel_in, vel), (w1_in, w1), (b1_in, b1), (w2_in, w2), (b2_in, b2), (w3_in, w3))
        )
    ]
    for load in loads:
        load.start()
    loads[0].wait()
    for c in range(3):
        for x in range(16):
            vb[c, pl.ds(8 + PLANE_ROWS * (x + 1), 16), :] = vel[c, x]

    def pack_faces(ref2d, which):
        lane = lanes((16, 128))
        packed = jnp.zeros((16, 128), F32)
        for c, load in enumerate(ref2d):
            sy[which, 0, c] = load(pl.ds(8 + PLANE_ROWS, 16, stride=PLANE_ROWS))
            sy[which, 1, c] = load(pl.ds(8 + PLANE_ROWS + 15, 16, stride=PLANE_ROWS))
            for x in range(16):
                plane = load(pl.ds(8 + PLANE_ROWS * (x + 1), 16))
                packed = jnp.where(lane // 2 == 4 * x + c, lane_roll(plane, 8 * x + 2 * c + 1), packed)
        sz[which] = packed

    pack_faces([lambda d, c=c: vb[c, d, :] for c in range(3)], 0)

    pl.semaphore_wait(barrier, len(FACES))

    low, high = 8, 8 + PLANE_ROWS * 17
    first, last = 8 + PLANE_ROWS, 8 + PLANE_ROWS * 16
    vel_copies = [
        cp.start(vel.at[:, 0], vb.at[:, pl.ds(high, 16), :], (-1, 0, 0)),
        cp.start(vel.at[:, 15], vb.at[:, pl.ds(low, 16), :], (1, 0, 0)),
        cp.start(sy.at[0, 0], rz.at[0, 1], (0, -1, 0)),
        cp.start(sy.at[0, 1], rz.at[0, 0], (0, 1, 0)),
        cp.start(sz.at[0], rz.at[0, 2, 1], (0, 0, -1)),
        cp.start(sz.at[0], rz.at[0, 2, 0], (0, 0, 1)),
    ]

    for load in loads[1:]:
        load.wait()
    spread = (rows_of((256, 32)) // 8 == lanes((256, 32))).astype(BF16)
    spread_t = (rows_of((32, 256)) == lanes((32, 256)) // 8).astype(BF16)
    columns = (rows_of((80, 9)) // 8 == lanes((80, 9))).astype(BF16)
    wide = lax.dot_general(
        spread, dot(columns, w1[...]).astype(BF16), (((1,), (1,)), ((), ())), preferred_element_type=F32
    )
    same = rows_of((256, 80)) % 8 == lanes((256, 80)) % 8
    w1k[...] = jnp.where(same, wide, 0.0).astype(BF16)
    wide = dot(dot(spread, w2[...]).astype(BF16), spread_t)
    same = rows_of((256, 256)) % 8 == lanes((256, 256)) % 8
    w2k[...] = jnp.where(same, wide, 0.0).astype(BF16)
    wide = jnp.broadcast_to(dot(w3[...], spread_t), (16, 256))
    same = rows_of((16, 256)) == lanes((16, 256)) % 8
    w3k[...] = jnp.where(same, wide, 0.0).astype(BF16)
    mine = rows_of((256, 32)) // 8 == lanes((256, 32))
    for bias, kept in ((b1, b1k), (b2, b2k)):
        column = jnp.sum(jnp.where(mine, bias[...], 0.0), axis=1, keepdims=True)
        kept[...] = jnp.broadcast_to(column, (256, 128))
    lb2[...] = jnp.zeros_like(lb2)

    for c in vel_copies:
        c.wait_recv()
    for c in range(3):
        vb[c, pl.ds(8 + PLANE_ROWS - 1, 16, stride=PLANE_ROWS), :] = rz[0, 0, c]
        vb[c, pl.ds(8 + PLANE_ROWS + 16, 16, stride=PLANE_ROWS), :] = rz[0, 1, c]

    lane16 = lanes((16, 128))

    def z_next(plane, halo, x, c):
        beyond = pltpu.roll(halo, (254 - 8 * x - 2 * c) % 128, 1)
        return jnp.where(lane16 == 127, beyond, lane_roll(plane, -1))

    def z_last(plane, halo, x, c):
        beyond = pltpu.roll(halo, (256 - 8 * x - 2 * c) % 128, 1)
        return jnp.where(lane16 == 0, beyond, lane_roll(plane, 1))

    def neighbours(load, x, base, which, c):
        plane = load(base)
        return plane, [
            (load(base + PLANE_ROWS), load(base - PLANE_ROWS)),
            (load(base + 1), load(base - 1)),
            (z_next(plane, rz[which, 2, 1], x, c), z_last(plane, rz[which, 2, 0], x, c)),
        ]

    def vel_load(c):
        return lambda base: vb[c, pl.ds(base, 16), :]

    for first_x in range(0, 16, 4):
        listing = [[] for _ in range(10)]
        for x in range(first_x, first_x + 4):
            base = 8 + PLANE_ROWS * (x + 1)
            g = []
            for c in range(3):
                _, around = neighbours(vel_load(c), x, base, 0, c)
                g.append([0.5 * (a - b) for a, b in around])
            entries = [
                g[0][0], g[1][1], g[2][2],
                0.5 * (g[0][1] + g[1][0]), 0.5 * (g[0][2] + g[2][0]), 0.5 * (g[1][2] + g[2][1]),
                0.5 * (g[0][1] - g[1][0]), 0.5 * (g[0][2] - g[2][0]), 0.5 * (g[1][2] - g[2][1]),
                jnp.zeros((16, 128), F32),
            ]
            for tiles, entry in zip(listing, entries):
                tiles += [entry[0:8], entry[8:16]]
        features = jnp.concatenate(
            [jnp.concatenate(tiles, axis=1) for tiles in listing], axis=0
        ).astype(BF16)
        bias = jnp.concatenate([b1k[...]] * 8, axis=1)
        hidden = jnp.tanh(dot(w1k[...], features) + bias).astype(BF16)
        bias = jnp.concatenate([b2k[...]] * 8, axis=1)
        second = jnp.tanh(dot(w2k[...], hidden) + bias).astype(BF16)
        s = dot(w3k[...], second)[0:8]
        soft = GAIN * (jnp.maximum(s, 0.0) + jnp.log1p(jnp.exp(-jnp.abs(s))))
        for k in range(8):
            row = 8 + PLANE_ROWS * (first_x + k // 2 + 1) + 8 * (k % 2)
            nb[pl.ds(row, 8), :] = soft[:, 128 * k : 128 * k + 128]

    pack_faces([lambda d: nb[d, :]], 1)
    visc_copies = [
        cp.start(nb.at[pl.ds(first, 16), :], nb.at[pl.ds(high, 16), :], (-1, 0, 0)),
        cp.start(nb.at[pl.ds(last, 16), :], nb.at[pl.ds(low, 16), :], (1, 0, 0)),
        cp.start(sy.at[1, 0, 0], rz.at[1, 1, 0], (0, -1, 0)),
        cp.start(sy.at[1, 1, 0], rz.at[1, 0, 0], (0, 1, 0)),
        cp.start(sz.at[1], rz.at[1, 2, 1], (0, 0, -1)),
        cp.start(sz.at[1], rz.at[1, 2, 0], (0, 0, 1)),
    ]
    for c in visc_copies:
        c.wait_recv()
    nb[pl.ds(8 + PLANE_ROWS - 1, 16, stride=PLANE_ROWS), :] = rz[1, 0, 0]
    nb[pl.ds(8 + PLANE_ROWS + 16, 16, stride=PLANE_ROWS), :] = rz[1, 1, 0]

    for x in range(16):
        base = 8 + PLANE_ROWS * (x + 1)
        mid, thick = neighbours(lambda r: nb[pl.ds(r, 16), :], x, base, 1, 0)
        thick = [(0.5 * (mid + a), 0.5 * (mid + b)) for a, b in thick]
        all_v = [neighbours(vel_load(c), x, base, 0, c) for c in range(3)]
        for i in range(3):
            center, around = all_v[i]
            change = 0.0
            for j in range(3):
                (up, down), (up_j, down_j) = around[j], all_v[j][1][j]
                change = change + thick[j][0] * (up - center) - thick[j][1] * (center - down)
                change = change - 0.5 * (up_j * up - down_j * down)
            pb[i, pl.ds(base, 16), :] = center + TIME_STEP * change

    sy[2, 0, 0] = pb[1, pl.ds(first, 16, stride=PLANE_ROWS), :]
    sy[2, 1, 0] = pb[1, pl.ds(first + 15, 16, stride=PLANE_ROWS), :]
    packed = jnp.zeros((16, 128), F32)
    for x in range(16):
        plane = pb[2, pl.ds(8 + PLANE_ROWS * (x + 1), 16), :]
        packed = jnp.where(lane16 // 2 == 4 * x, lane_roll(plane, 8 * x + 1), packed)
    sz[2] = packed
    prov_copies = [
        cp.start(pb.at[0, pl.ds(first, 16), :], pb.at[0, pl.ds(high, 16), :], (-1, 0, 0)),
        cp.start(pb.at[0, pl.ds(last, 16), :], pb.at[0, pl.ds(low, 16), :], (1, 0, 0)),
        cp.start(sy.at[2, 0, 0], rz.at[2, 1, 0], (0, -1, 0)),
        cp.start(sy.at[2, 1, 0], rz.at[2, 0, 0], (0, 1, 0)),
        cp.start(sz.at[2], rz.at[2, 2, 1], (0, 0, -1)),
        cp.start(sz.at[2], rz.at[2, 2, 0], (0, 0, 1)),
    ]
    for c in prov_copies:
        c.wait_recv()
    pb[1, pl.ds(first - 1, 16, stride=PLANE_ROWS), :] = rz[2, 0, 0]
    pb[1, pl.ds(first + 16, 16, stride=PLANE_ROWS), :] = rz[2, 1, 0]

    for x in range(16):
        base = 8 + PLANE_ROWS * (x + 1)
        plane = pb[2, pl.ds(base, 16), :]
        total = pb[0, pl.ds(base + PLANE_ROWS, 16), :] - pb[0, pl.ds(base - PLANE_ROWS, 16), :]
        total = total + pb[1, pl.ds(base + 1, 16), :] - pb[1, pl.ds(base - 1, 16), :]
        beyond = jnp.where(lane16 == 127, lane_roll(rz[2, 2, 1], 126 - 8 * x), lane_roll(plane, -1))
        before = jnp.where(lane16 == 0, lane_roll(rz[2, 2, 0], -8 * x), lane_roll(plane, 1))
        dv[x] = 0.5 * (total + (beyond - before))

    for half in range(2):
        packed = jnp.zeros((16, 128), F32)
        for k in range(8):
            packed = jnp.where(lane16 // 16 == k, lane_roll(dv[8 * half + k], 16 * k + 8), packed)
        sdz[half] = packed
    div_copies = []
    for dx, dy, dz in AROUND:
        here_x, here_y = (1 - dx) // 2, (1 - dy) // 2
        if dz == 0:
            if dy == 0:
                src, dst = dv.at[pl.ds(10 if dx > 0 else 0, 6)], rdx.at[here_x]
            elif dx == 0:
                src, dst = dv.at[:, pl.ds(8 if dy > 0 else 0, 8), :], rdy.at[here_y]
            else:
                src = dv.at[pl.ds(10 if dx > 0 else 0, 6), pl.ds(8 if dy > 0 else 0, 8), :]
                dst = rde.at[here_x, here_y]
        else:
            half = pl.ds(0, 2) if dx == 0 else pl.ds(1 if dx > 0 else 0, 1)
            slot = pl.ds(1, 2) if dx == 0 else pl.ds(0 if dx > 0 else 3, 1)
            part = pl.ds(0, 16) if dy == 0 else pl.ds(8 if dy > 0 else 0, 8)
            rows = pl.ds(8, 16) if dy == 0 else pl.ds(0 if dy > 0 else 24, 8)
            src, dst = sdz.at[half, part, :], rdz.at[(1 - dz) // 2, slot, rows, :]
        div_copies.append(cp.start(src, dst, (dx, dy, dz)))

    def at0(p):
        return 8 + 32 * p

    for x in range(16):
        db[0, pl.ds(at0(x + 6) + 8, 16), :] = dv[x]
    for c in div_copies:
        c.wait_recv()
    for x in range(6):
        for side, p in ((0, x), (1, 22 + x)):
            db[0, pl.ds(at0(p) + 8, 16), :] = rdx[side, x]
            db[0, pl.ds(at0(p), 8), :] = rde[side, 0, x]
            db[0, pl.ds(at0(p) + 24, 8), :] = rde[side, 1, x]
    for x in range(16):
        db[0, pl.ds(at0(x + 6), 8), :] = rdy[0, x]
        db[0, pl.ds(at0(x + 6) + 24, 8), :] = rdy[1, x]
    lane32 = lanes((32, 128))
    for g in range(4):
        both = jnp.where(lane32 % 16 < 8, rdz[0, g], rdz[1, g])
        for k in range(8):
            x = 8 * (g - 1) + k
            if -6 <= x < 22:
                db[1, pl.ds(at0(x + 6), 32), :] = lane_roll(both, -(16 * k + 8))

    for p in range(1, 27, 2):
        b, around = sum6_wide(db, at0(p), 64, 32)
        for t in (0, 1):
            v0[t, pl.ds(at0(p), 64), :] = -C * (1.2 * b[t] + C * around[t])
    for k in range(12):
        base = at0(2 + 2 * k)
        v, around = sum6_wide(v0, base, 64, 32)
        for t in (0, 1):
            residual = db[t, pl.ds(base, 64), :] - (around[t] - 6.0 * v[t])
            rs[pl.ds(32 * k, 32), pl.ds(128 * t, 128)] = residual[0:32] + residual[32:64]
    halve = jnp.where(coarse_lane((256, 128), 0) == lanes((256, 128)), 0.125, 0.0).astype(F32)
    rt[...] = dot(rs[...], halve, EXACT)
    s1[...] = rt[pl.ds(0, 192, stride=2), :] + rt[pl.ds(1, 192, stride=2), :]

    lane8 = lanes((8, 128))
    packed = jnp.zeros((8, 128), F32)
    for x in range(8):
        plane = s1[pl.ds(16 * (x + 2) + 4, 8), :]
        r1c[x] = plane
        packed = jnp.where(lane8 // 8 == 2 * x, lane_roll(plane, 16 * x - 88), packed)
        packed = jnp.where(lane8 // 8 == 2 * x + 1, lane_roll(plane, 16 * x + 8 - 32), packed)
    sez[...] = packed

    for p in range(1, 11, 5):
        b, around = sum6(s1, 16 * p, 80, 16)
        v1s[pl.ds(16 * p, 80), :] = -4.0 * C * (1.2 * b + C * around)
    parts = []
    for k in range(4):
        base = 16 * (2 + 2 * k)
        v, around = sum6(v1s, base, 32, 16)
        residual = s1[pl.ds(base, 32), :] - 0.25 * (around - 6.0 * v)
        parts.append(residual[0:16] + residual[16:32])
    halve = halve[0:128]
    rt[pl.ds(0, 64), :] = dot(jnp.concatenate(parts, axis=0), halve, EXACT)
    packed = jnp.zeros((8, 128), F32)
    for x in range(4):
        plane = rt[pl.ds(16 * x, 8, stride=2), :] + rt[pl.ds(16 * x + 1, 8, stride=2), :]
        packed = jnp.where(lane8 // 32 == x, lane_roll(plane, 32 * x - 48), packed)
    sa[...] = packed
    ra[3, 1] = packed
    xz_copies = [
        cp.start(sa, ra.at[3 - dx, 1 - dz], (dx, 0, dz))
        for dx in range(-3, 4)
        for dz in (-1, 0, 1)
        if (dx, dz) != (0, 0)
    ]
    src_copies = []
    for dx, dy, dz in AROUND:
        here_x, here_y = (1 - dx) // 2, (1 - dy) // 2
        if dz == 0:
            planes = pl.ds(3 if dx > 0 else 0, 5)
            if dy == 0:
                src, dst = r1c.at[planes], rex.at[here_x]
            elif dx == 0:
                src, dst = r1c, rey.at[here_y]
            else:
                src, dst = r1c.at[planes], ree.at[here_x, here_y]
        else:
            src, dst = sez, rez.at[(1 - dz) // 2, 1 - dx, pl.ds(8 * (1 - dy), 8), :]
        src_copies.append(cp.start(src, dst, (dx, dy, dz)))

    for c in xz_copies:
        c.wait_recv()
    row8 = rows_of((8, 128))
    kept_rows = (row8 >= 2) & (row8 < 6)
    for dx in range(7):
        four = []
        for x in range(4):
            before, here, after = (
                lane_roll(ra[dx, k], lane - 32 * x) for k, lane in ((0, 16), (1, 48), (2, 80))
            )
            whole = jnp.where(lane8 < 48, before, jnp.where(lane8 < 80, here, after))
            lb2[pl.ds(32 * (4 * dx + x) + 12, 4), :] = whole[2:6]
            four.append(whole)
        pairs = [
            jnp.where(lane8 < 64, lane_roll(four[i], -32), lane_roll(four[i + 1], 32)) for i in (0, 2)
        ]
        sb[dx] = jnp.where(kept_rows, pairs[0], pltpu.roll(pairs[1], 4, 0))
    y_copies = []
    for dy in (1, -1, 2, -2, 3, -3):
        wanted = pl.ds(abs(dy) - 1, 9 - 2 * abs(dy))
        y_copies.append(cp.start(sb.at[wanted], rb.at[3 - dy, wanted], (0, dy, 0)))

    for c in src_copies:
        c.wait_recv()
    lane24 = lanes((24, 128))
    for p in range(18):
        dx, x = (p - 5) // 8, (p - 5) % 8
        if dx == 0:
            three = [rey[0, x], r1c[x], rey[1, x]]
        else:
            side = (dx + 1) // 2
            k = x - 3 if dx < 0 else x
            three = [ree[side, 0, k], rex[side, k], ree[side, 1, k]]
        before = lane_roll(rez[0, dx + 1], 24 - 16 * x)
        after = lane_roll(rez[1, dx + 1], 96 - 16 * x - 8)
        here = jnp.concatenate(three, axis=0)
        lb1[pl.ds(24 * p, 24), :] = jnp.where(
            lane24 < 32, before, jnp.where(lane24 < 96, here, after)
        )
    for p in range(1, 17, 4):
        b, around = sum6(lb1, 24 * p, 96, 24)
        v1[pl.ds(24 * p, 96), :] = -4.0 * C * (1.2 * b + C * around)

    for c in y_copies:
        c.wait_recv()
    for dy in (-3, -2, -1, 1, 2, 3):
        for dx in range(abs(dy) - 1, 8 - abs(dy)):
            tile = rb[3 + dy, dx]
            other = pltpu.roll(tile, 4, 0)
            for x in range(4):
                plane = lane_roll(tile if x < 2 else other, 32 if x % 2 == 0 else -32)
                lb2[pl.ds(32 * (4 * dx + x) + 12 + 4 * dy, 4), :] = plane[2:6]

    for p in range(1, 27, 2):
        b, around = sum6(lb2, 32 * p, 64, 32)
        v2[pl.ds(32 * p, 64), :] = -16.0 * C * (1.2 * b + C * around)
    for k in range(12):
        base = 32 * (2 + 2 * k)
        v, around = sum6(v2, base, 64, 32)
        residual = lb2[pl.ds(base, 64), :] - 0.0625 * (around - 6.0 * v)
        rs[pl.ds(32 * k, 32), pl.ds(0, 128)] = residual[0:32] + residual[32:64]
    rt[...] = dot(rs[:, 0:128], halve, EXACT)
    lb3[...] = rt[pl.ds(0, 192, stride=2), :] + rt[pl.ds(1, 192, stride=2), :]

    b, around = sum6(lb3, 16, 160, 16)
    v3[pl.ds(16, 160), :] = -64.0 * C * (1.2 * b + C * around)
    v, around = sum6(v3, 32, 128, 16)
    u3[pl.ds(32, 128), :] = 0.2 * v + C * around - 64.0 * C * lb3[pl.ds(32, 128), :]
    v, around = sum6(u3, 48, 96, 16)
    coarse = 0.2 * v + C * around - 64.0 * C * lb3[pl.ds(48, 96), :]

    double = jnp.where(rows_of((128, 256)) == coarse_lane((128, 256), 1), 1.0, 0.0).astype(F32)
    fine = dot(coarse, double[:, 0:128], EXACT)
    for k in range(6):
        for p in (8 + 2 * k, 9 + 2 * k):
            for odd in (0, 1):
                where = pl.ds(32 * p + odd, 16, stride=2)
                v2[where, :] = v2[where, :] + fine[16 * k : 16 * k + 16]
    for p in range(9, 19, 2):
        v, around = sum6(v2, 32 * p, 64, 32)
        u2[pl.ds(32 * p, 64), :] = 0.2 * v + C * around - 16.0 * C * lb2[pl.ds(32 * p, 64), :]
    for k in range(4):
        base = 32 * (10 + 2 * k)
        v, around = sum6(u2, base, 64, 32)
        rs[pl.ds(64 * k, 64), pl.ds(0, 128)] = (
            0.2 * v + C * around - 16.0 * C * lb2[pl.ds(base, 64), :]
        )

    fine = dot(rs[0:256, 0:128], double[:, 0:128], EXACT)
    for k in range(8):
        for p in (1 + 2 * k, 2 + 2 * k):
            for odd in (0, 1):
                where = pl.ds(24 * p + odd, 12, stride=2)
                v1[where, :] = v1[where, :] + fine[32 * k + 8 : 32 * k + 20]
    for p in range(2, 16, 2):
        v, around = sum6(v1, 24 * p, 48, 24)
        u1[pl.ds(24 * p, 48), :] = 0.2 * v + C * around - 4.0 * C * lb1[pl.ds(24 * p, 48), :]
    for k in range(6):
        base = 24 * (3 + 2 * k)
        v, around = sum6(u1, base, 48, 24)
        rs[pl.ds(48 * k, 48), pl.ds(0, 128)] = (
            0.2 * v + C * around - 4.0 * C * lb1[pl.ds(base, 48), :]
        )

    for t in (0, 1):
        fine = dot(rs[0:288, 0:128], double[:, 128 * t : 128 * t + 128], EXACT)
        for k in range(12):
            for p in (2 + 2 * k, 3 + 2 * k):
                for odd in (0, 1):
                    where = pl.ds(at0(p) + odd, 16, stride=2)
                    v0[t, where, :] = v0[t, where, :] + fine[24 * k + 4 : 24 * k + 20]
    for p in range(4, 24, 2):
        v, around = sum6_wide(v0, at0(p), 64, 32)
        for t in (0, 1):
            b = db[t, pl.ds(at0(p), 64), :]
            u0[t, pl.ds(at0(p), 64), :] = 0.2 * v[t] + C * around[t] - C * b
    for p in range(5, 23, 2):
        v, around = sum6_wide(u0, at0(p), 64, 32)
        for t in (0, 1):
            b = db[t, pl.ds(at0(p), 64), :]
            v0[t, pl.ds(at0(p), 64), :] = 0.2 * v[t] + C * around[t] - C * b

    for x in range(16):
        base = at0(x + 6) + 8
        here, beyond = v0[0, pl.ds(base, 16), :], v0[1, pl.ds(base, 16), :]
        pout[x] = here
        slopes = [
            v0[0, pl.ds(base + 32, 16), :] - v0[0, pl.ds(base - 32, 16), :],
            v0[0, pl.ds(base + 1, 16), :] - v0[0, pl.ds(base - 1, 16), :],
            jnp.where(lane16 == 127, lane_roll(beyond, -1), lane_roll(here, -1))
            - jnp.where(lane16 == 0, lane_roll(beyond, 1), lane_roll(here, 1)),
        ]
        for c in range(3):
            vout[c, x] = pb[c, pl.ds(8 + PLANE_ROWS * (x + 1), 16), :] - 0.5 * slopes[c]

    for c in cp.made:
        c.wait_send()


def body(velocity, input_weight, input_bias, hidden_weight, hidden_bias, output_weight):
    def scratch(*shape):
        return pltpu.VMEM(shape, F32)

    plane_buffer = 16 + PLANE_ROWS * 18
    level0 = 16 + 32 * 28
    return pl.pallas_call(
        kernel,
        out_shape=(
            pltpu.VMEM((3, 16, 16, 128), F32),
            pltpu.VMEM((16, 16, 128), F32),
        ),
        in_specs=[pl.BlockSpec(memory_space=pltpu.HBM)] * 6,
        out_specs=[pl.BlockSpec(memory_space=pltpu.VMEM)] * 2,
        scratch_shapes=[
            scratch(3, 16, 16, 128),
            pltpu.VMEM((9, 32), BF16),
            scratch(1, 32),
            pltpu.VMEM((32, 32), BF16),
            scratch(1, 32),
            pltpu.VMEM((1, 32), BF16),
            pltpu.VMEM((256, 80), BF16),
            pltpu.VMEM((256, 256), BF16),
            pltpu.VMEM((16, 256), BF16),
            scratch(256, 128),
            scratch(256, 128),
            scratch(3, plane_buffer, 128),
            scratch(plane_buffer, 128),
            scratch(3, plane_buffer, 128),
            scratch(3, 2, 3, 16, 128),
            scratch(3, 16, 128),
            scratch(3, 3, 3, 16, 128),
            scratch(16, 16, 128),
            scratch(2, 16, 128),
            scratch(2, 6, 16, 128),
            scratch(2, 16, 8, 128),
            scratch(2, 2, 6, 8, 128),
            scratch(2, 4, 32, 128),
            scratch(2, level0, 128),
            scratch(2, level0, 128),
            scratch(2, level0, 128),
            scratch(384, 256),
            scratch(384, 128),
            scratch(192, 128),
            scratch(192, 128),
            scratch(8, 8, 128),
            scratch(8, 128),
            scratch(2, 5, 8, 128),
            scratch(2, 8, 8, 128),
            scratch(2, 2, 5, 8, 128),
            scratch(2, 3, 24, 128),
            scratch(432, 128),
            scratch(432, 128),
            scratch(432, 128),
            scratch(8, 128),
            scratch(7, 3, 8, 128),
            scratch(7, 8, 128),
            scratch(7, 7, 8, 128),
            scratch(896, 128),
            scratch(896, 128),
            scratch(896, 128),
            scratch(192, 128),
            scratch(192, 128),
            scratch(192, 128),
            pltpu.SemaphoreType.DMA((N_COPIES,)),
            pltpu.SemaphoreType.DMA((N_COPIES,)),
            pltpu.SemaphoreType.DMA((6,)),
        ],
        compiler_params=pltpu.CompilerParams(
            collective_id=0, has_side_effects=True, vmem_limit_bytes=60 * 1024 * 1024
        ),
    )(
        velocity,
        input_weight.T,
        input_bias.reshape(1, 32),
        hidden_weight,
        hidden_bias.reshape(1, 32),
        output_weight.reshape(1, 32),
    )


def solution(mesh):
    return jax.shard_map(
        body,
        mesh=mesh,
        in_specs=(P(None, "gx", "gy", "gz"), P(), P(), P(), P(), P()),
        out_specs=(P(None, "gx", "gy", "gz"), P("gx", "gy", "gz")),
        check_vma=False,
    )
```

```python
import jax
import jax.numpy as jnp
from jax import lax
from jax.experimental import pallas as pl
from jax.experimental.pallas import tpu as pltpu
from jax.sharding import PartitionSpec as P

MESH = pl.DeviceIdType.MESH
AXES = ("gx", "gy", "gz")
F32, BF16 = jnp.float32, jnp.bfloat16

TIME_STEP = 0.1
GAIN = 0.5
C = 0.8 / 6.0

FACES = [(1, 0, 0), (-1, 0, 0), (0, 1, 0), (0, -1, 0), (0, 0, 1), (0, 0, -1)]
AROUND = [
    (i, j, k) for i in (-1, 0, 1) for j in (-1, 0, 1) for k in (-1, 0, 1) if (i, j, k) != (0, 0, 0)
]
PLANE_ROWS = 24
NEAR = [(a, b) for a in range(5) for b in range(5) if a + b <= 4]
CORNER = [(i, j, k, o) for i in (0, 1) for j in (0, 1) for k, o in enumerate(NEAR)]
EDGES = [o for o in AROUND if abs(o[0]) + abs(o[1]) + abs(o[2]) == 2]
N_COPIES = 6 + 16 + 20 + 26 * 2 + 20 + 6


def at(x, y=0):
    return 8 + PLANE_ROWS * (x + 2) + y


def column(y):
    return pl.ds(at(0, y), 16, stride=PLANE_ROWS)


def at0(p):
    return 8 + 32 * p


def lanes(shape):
    return lax.broadcasted_iota(jnp.int32, shape, len(shape) - 1)


def rows_of(shape):
    return lax.broadcasted_iota(jnp.int32, shape, len(shape) - 2)


def lane_roll(value, shift):
    return pltpu.roll(value, shift % 128, value.ndim - 1)


def dot(a, b, precision=None):
    return jnp.dot(a, b, precision=precision, preferred_element_type=F32)


def coarse_lane(shape, axis):
    fine = lax.broadcasted_iota(jnp.int32, shape, axis)
    return jnp.where(fine < 192, 32 + fine // 2, fine // 2 - 96)


def exact_dot(a, b):
    b = b.astype(BF16)
    first = a.astype(BF16)
    rest = a - first.astype(F32)
    second = rest.astype(BF16)
    third = (rest - second.astype(F32)).astype(BF16)
    return dot(third, b) + dot(second, b) + dot(first, b)


class Copies:
    def __init__(self, ids, send_sem, recv_sem):
        self.ids, self.send_sem, self.recv_sem = ids, send_sem, recv_sem
        self.made, self.count = [], 0

    def device(self, offset):
        return tuple(lax.rem(i + 8 + o, 8) for i, o in zip(self.ids, offset))

    def start(self, src, dst, offset):
        k = self.count + len(self.made)
        copy = pltpu.make_async_remote_copy(
            src_ref=src,
            dst_ref=dst,
            send_sem=self.send_sem.at[k],
            recv_sem=self.recv_sem.at[k],
            device_id=self.device(offset),
            device_id_type=MESH,
        )
        copy.start()
        self.made.append(copy)
        return copy

    def sent(self):
        for copy in self.made:
            copy.wait_send()
        self.count += len(self.made)
        self.made = []


def sum6(ref, base, n, period):
    center = ref[pl.ds(base, n), :]
    total = ref[pl.ds(base + period, n), :] + ref[pl.ds(base - period, n), :]
    total = total + ref[pl.ds(base + 1, n), :] + ref[pl.ds(base - 1, n), :]
    return center, total + lane_roll(center, 1) + lane_roll(center, -1)


def sum6_wide(ref, base, n, period):
    center = [ref[t, pl.ds(base, n), :] for t in (0, 1)]
    lane = lanes((n, 128))
    up = [lane_roll(c, -1) for c in center]
    down = [lane_roll(c, 1) for c in center]
    out = []
    for t in (0, 1):
        total = ref[t, pl.ds(base + period, n), :] + ref[t, pl.ds(base - period, n), :]
        total = total + ref[t, pl.ds(base + 1, n), :] + ref[t, pl.ds(base - 1, n), :]
        total = total + jnp.where(lane == 127, up[1 - t], up[t])
        out.append(total + jnp.where(lane == 0, down[1 - t], down[t]))
    return center, out


def kernel(
    vel_in, w1_in, b1_in, w2_in, b2_in, w3_in, vout, pout,
    vel, w1, b1, w2, b2, w3, w1k, w2k, w3k, b1k, b2k,
    vb, nb, pb, sy, sz, sxy, ry, rz, rxy, rxz, syn, szn, sxyn, ryn, rxyn, cz, zb,
    dv, dvr, sdy, sde, sdz, rdx, rdy, rde, rdz, db, v0, u0,
    rs, rt, s1, v1s, r1c, sez, rex, rey, ree, rez, lb1, v1, u1,
    sa, ra, sb, rb, lb2, v2, u2, lb3, v3, u3,
    send_sem, recv_sem, load_sem,
):
    ids = [lax.axis_index(a) for a in AXES]
    cp = Copies(ids, send_sem, recv_sem)
    barrier = pltpu.get_barrier_semaphore()
    for offset in FACES:
        pl.semaphore_signal(barrier, inc=1, device_id=cp.device(offset), device_id_type=MESH)

    loads = [
        pltpu.make_async_copy(src, dst, load_sem.at[k])
        for k, (src, dst) in enumerate(
            ((vel_in, vel), (w1_in, w1), (b1_in, b1), (w2_in, w2), (b2_in, b2), (w3_in, w3))
        )
    ]
    for load in loads:
        load.start()
    loads[0].wait()
    for c in range(3):
        for x in range(16):
            vb[c, pl.ds(at(x), 16), :] = vel[c, x]

    lane16 = lanes((16, 128))

    def pack_z(plane_of):
        packed = jnp.zeros((16, 128), F32)
        for x in range(16):
            plane = plane_of(x)
            packed = jnp.where(lane16 // 2 == 4 * x + 1, lane_roll(plane, 8 * x + 2), packed)
            packed = jnp.where(lane16 // 2 == 4 * x + 2, lane_roll(plane, 8 * x + 6), packed)
        return packed

    for c in range(3):
        for k, y in enumerate((0, 1, 14, 15)):
            sy[k, c] = vb[c, column(y), :]
        sz[c] = pack_z(lambda x: vel[c, x])
        for i in (0, 1):
            for j in (0, 1):
                sxy[i, j, pl.ds(c, 1), :] = vel[c, 15 * i, pl.ds(15 * j, 1), :]

    pl.semaphore_wait(barrier, len(FACES))

    vel_copies = [
        cp.start(sz, rz.at[0, pl.ds(0, 3), pl.ds(8, 16), :], (0, 0, 1)),
        cp.start(sz, rz.at[1, pl.ds(0, 3), pl.ds(8, 16), :], (0, 0, -1)),
        cp.start(sy.at[3], ry.at[1], (0, 1, 0)),
        cp.start(sy.at[0], ry.at[2], (0, -1, 0)),
        cp.start(vel.at[:, 15], vb.at[:, pl.ds(at(-1), 16), :], (1, 0, 0)),
        cp.start(vel.at[:, 0], vb.at[:, pl.ds(at(16), 16), :], (-1, 0, 0)),
    ]

    for load in loads[1:]:
        load.wait()
    spread = (rows_of((256, 32)) // 8 == lanes((256, 32))).astype(BF16)
    spread_t = (rows_of((32, 256)) == lanes((32, 256)) // 8).astype(BF16)
    columns = (rows_of((80, 9)) // 8 == lanes((80, 9))).astype(BF16)
    wide = lax.dot_general(
        spread, dot(columns, w1[...]).astype(BF16), (((1,), (1,)), ((), ())), preferred_element_type=F32
    )
    same = rows_of((256, 80)) % 8 == lanes((256, 80)) % 8
    w1k[...] = jnp.where(same, wide, 0.0).astype(BF16)
    wide = dot(dot(spread, w2[...]).astype(BF16), spread_t)
    same = rows_of((256, 256)) % 8 == lanes((256, 256)) % 8
    w2k[...] = jnp.where(same, wide, 0.0).astype(BF16)
    wide = jnp.broadcast_to(dot(w3[...], spread_t), (16, 256))
    same = rows_of((16, 256)) == lanes((16, 256)) % 8
    w3k[...] = jnp.where(same, wide, 0.0).astype(BF16)
    mine = rows_of((256, 32)) // 8 == lanes((256, 32))
    for bias, kept in ((b1, b1k), (b2, b2k)):
        bias_column = jnp.sum(jnp.where(mine, bias[...], 0.0), axis=1, keepdims=True)
        kept[...] = jnp.broadcast_to(bias_column, (256, 128))
    lb2[...] = jnp.zeros_like(lb2)
    for p in range(28):
        for first in (0, 24):
            db[0, pl.ds(at0(p) + first, 8), :] = jnp.zeros((8, 128), F32)
    for c in vel_copies:
        c.wait_recv()
    for c in range(3):
        vb[c, column(-1), :] = ry[1, c]
        vb[c, column(16), :] = ry[2, c]

    more_copies = []
    for dx, dy, dz in EDGES:
        i, j, k = (1 - dx) // 2, (1 - dy) // 2, (1 - dz) // 2
        if dz == 0:
            src, dst = sxy.at[1 - i, 1 - j], rxy.at[i, j]
        elif dy == 0:
            src, dst = sz, rxz.at[k, i, pl.ds(0, 3)]
        else:
            part, rows = pl.ds(8 * (1 - j), 8), pl.ds(24 * j, 8)
            src, dst = sz.at[:, part, :], rz.at[k, pl.ds(0, 3), rows, :]
        more_copies.append(cp.start(src, dst, (dx, dy, dz)))
    more_copies += [
        cp.start(sy.at[2], ry.at[0], (0, 1, 0)),
        cp.start(sy.at[1], ry.at[3], (0, -1, 0)),
        cp.start(vel.at[:, 14], vb.at[:, pl.ds(at(-2), 16), :], (1, 0, 0)),
        cp.start(vel.at[:, 1], vb.at[:, pl.ds(at(17), 16), :], (-1, 0, 0)),
    ]

    for first_x in range(0, 16, 4):
        listing = [[] for _ in range(10)]
        for x in range(first_x, first_x + 4):
            base = at(x)
            g = []
            for c in range(3):
                plane = vb[c, pl.ds(base, 16), :]
                after = lane_roll(rz[1, c, pl.ds(8, 16), :], 125 - 8 * x)
                before = lane_roll(rz[0, c, pl.ds(8, 16), :], -(8 * x + 5))
                after = jnp.where(lane16 == 127, after, lane_roll(plane, -1))
                before = jnp.where(lane16 == 0, before, lane_roll(plane, 1))
                around = [
                    (vb[c, pl.ds(base + step, 16), :], vb[c, pl.ds(base - step, 16), :])
                    for step in (PLANE_ROWS, 1)
                ]
                g.append([0.5 * (a - b) for a, b in around + [(after, before)]])
            entries = [
                g[0][0], g[1][1], g[2][2],
                0.5 * (g[0][1] + g[1][0]), 0.5 * (g[0][2] + g[2][0]), 0.5 * (g[1][2] + g[2][1]),
                0.5 * (g[0][1] - g[1][0]), 0.5 * (g[0][2] - g[2][0]), 0.5 * (g[1][2] - g[2][1]),
                jnp.zeros((16, 128), F32),
            ]
            for tiles, entry in zip(listing, entries):
                tiles += [entry[0:8], entry[8:16]]
        features = jnp.concatenate(
            [jnp.concatenate(tiles, axis=1) for tiles in listing], axis=0
        ).astype(BF16)
        bias = jnp.concatenate([b1k[...]] * 8, axis=1)
        hidden = jnp.tanh(dot(w1k[...], features) + bias).astype(BF16)
        bias = jnp.concatenate([b2k[...]] * 8, axis=1)
        second = jnp.tanh(dot(w2k[...], hidden) + bias).astype(BF16)
        s = dot(w3k[...], second)[0:8]
        soft = GAIN * (jnp.maximum(s, 0.0) + jnp.log1p(jnp.exp(-jnp.abs(s))))
        for k in range(8):
            nb[pl.ds(at(first_x + k // 2, 8 * (k % 2)), 8), :] = soft[:, 128 * k : 128 * k + 128]

    for k, y in enumerate((0, 1, 14, 15)):
        syn[k] = nb[column(y), :]
    szn[...] = pack_z(lambda x: nb[pl.ds(at(x), 16), :])
    for i in (0, 1):
        for j in (0, 1):
            sxyn[i, j, pl.ds(0, 1), :] = nb[pl.ds(at(15 * i, 15 * j), 1), :]
    visc_copies = []
    for dx, dy, dz in EDGES:
        i, j, k = (1 - dx) // 2, (1 - dy) // 2, (1 - dz) // 2
        if dz == 0:
            src, dst = sxyn.at[1 - i, 1 - j], rxyn.at[i, j]
        elif dy == 0:
            src, dst = szn, rxz.at[k, i, 3]
        else:
            part, rows = pl.ds(8 * (1 - j), 8), pl.ds(24 * j, 8)
            src, dst = szn.at[part, :], rz.at[k, 3, rows, :]
        visc_copies.append(cp.start(src, dst, (dx, dy, dz)))
    visc_copies += [
        cp.start(szn, rz.at[0, 3, pl.ds(8, 16), :], (0, 0, 1)),
        cp.start(szn, rz.at[1, 3, pl.ds(8, 16), :], (0, 0, -1)),
        cp.start(syn.at[pl.ds(2, 2)], ryn.at[pl.ds(0, 2)], (0, 1, 0)),
        cp.start(syn.at[pl.ds(0, 2)], ryn.at[pl.ds(2, 2)], (0, -1, 0)),
    ]
    for x in (14, 15):
        here, there = pl.ds(at(x), 16), pl.ds(at(x - 16), 16)
        visc_copies.append(cp.start(nb.at[here, :], nb.at[there, :], (1, 0, 0)))
    for x in (0, 1):
        here, there = pl.ds(at(x), 16), pl.ds(at(x + 16), 16)
        visc_copies.append(cp.start(nb.at[here, :], nb.at[there, :], (-1, 0, 0)))

    slot = lanes((32, 128)) % 8

    def beyond(f, own):
        none = jnp.zeros((8, 128), F32)
        whole = jnp.concatenate([none, own, none], axis=0)
        outer = jnp.where(slot < 4, lane_roll(rz[0, f], -4), lane_roll(rz[1, f], 4))
        whole = jnp.where((slot >= 2) & (slot < 6), whole, outer)
        cz[f] = whole
        ends = jnp.where(slot == 0, lane_roll(whole, -1), lane_roll(whole, -5))
        for x in range(16):
            zb[f, pl.ds(at(x, -4), 24), :] = lane_roll(ends, -(8 * x + 1))[4:28]
        zb[f, pl.ds(at(-1), 16), :] = jnp.where(
            lane16 == 127, lane_roll(rxz[0, 0, f], 2), lane_roll(rxz[1, 0, f], 6)
        )
        zb[f, pl.ds(at(16), 16), :] = jnp.where(
            lane16 == 127, lane_roll(rxz[0, 1, f], 122), lane_roll(rxz[1, 1, f], -2)
        )

    for c in more_copies:
        c.wait_recv()
    for c in range(3):
        vb[c, column(-2), :] = ry[0, c]
        vb[c, column(17), :] = ry[3, c]
        for i in (0, 1):
            for j in (0, 1):
                vb[c, pl.ds(at(17 * i - 1, 17 * j - 1), 1), :] = rxy[i, j, pl.ds(c, 1), :]
        beyond(c, sz[c])
    for c in visc_copies:
        c.wait_recv()
    for k, y in enumerate((-2, -1, 16, 17)):
        nb[column(y), :] = ryn[k]
    for i in (0, 1):
        for j in (0, 1):
            nb[pl.ds(at(17 * i - 1, 17 * j - 1), 1), :] = rxyn[i, j, pl.ds(0, 1), :]
    beyond(3, szn[...])

    def change(i, n_mid, n_near, v_mid, v_near):
        total = 0.0
        for j in range(3):
            (up, down), (up_j, down_j) = v_near[i][j], v_near[j][j]
            total = total + 0.5 * (n_mid + n_near[j][0]) * (up - v_mid[i])
            total = total - 0.5 * (n_mid + n_near[j][1]) * (v_mid[i] - down)
            total = total - 0.5 * (up_j * up - down_j * down)
        return v_mid[i] + TIME_STEP * total

    def near(load, ends, start, n):
        mid = load(start)
        lane = lanes((n, 128))
        return mid, [
            (load(start + PLANE_ROWS), load(start - PLANE_ROWS)),
            (load(start + 1), load(start - 1)),
            (
                lane_roll(jnp.where(lane == 0, ends, mid), -1),
                lane_roll(jnp.where(lane == 127, ends, mid), 1),
            ),
        ]

    def tendency(start, n, components):
        where = pl.ds(start, n)
        n_mid, n_near = near(lambda r: nb[pl.ds(r, n), :], zb[3, where, :], start, n)
        both = [near(lambda r, c=c: vb[c, pl.ds(r, n), :], zb[c, where, :], start, n) for c in range(3)]
        for i in components:
            pb[i, where, :] = change(i, n_mid, n_near, [b[0] for b in both], [b[1] for b in both])

    for x in range(16):
        tendency(at(x), 16, (0, 1, 2))
    tendency(at(-1), 16, (0,))
    tendency(at(16), 16, (0,))
    for x in range(-1, 16):
        tendency(at(x, 16), 8, (1,))

    def near_end(f):
        mid = cz[f, pl.ds(8, 16), :]
        above = jnp.where(lane16 == 126, lane_roll(rxz[1, 1, f], 124), lane_roll(rxz[0, 1, f], 116))
        below = jnp.where(lane16 == 6, lane_roll(rxz[1, 0, f], 12), lane_roll(rxz[0, 0, f], 4))
        return mid, [
            (
                jnp.where(lane16 >= 120, above, lane_roll(mid, -8)),
                jnp.where(lane16 < 8, below, lane_roll(mid, 8)),
            ),
            (cz[f, pl.ds(9, 16), :], cz[f, pl.ds(7, 16), :]),
            (lane_roll(mid, -1), lane_roll(mid, 1)),
        ]

    fields = [near_end(f) for f in range(4)]
    far = change(2, *fields[3], [f[0] for f in fields[:3]], [f[1] for f in fields[:3]])
    far = jnp.where(lane16 % 8 == 0, lane_roll(far, -1), lane_roll(far, -5))

    for x in range(16):
        base = at(x)
        plane, ends = pb[2, pl.ds(base, 16), :], lane_roll(far, -(8 * x + 1))
        total = pb[0, pl.ds(base + PLANE_ROWS, 16), :] - pb[0, pl.ds(base - PLANE_ROWS, 16), :]
        total = total + pb[1, pl.ds(base + 1, 16), :] - pb[1, pl.ds(base - 1, 16), :]
        total = total + lane_roll(jnp.where(lane16 == 0, ends, plane), -1)
        dv[x] = 0.5 * (total - lane_roll(jnp.where(lane16 == 127, ends, plane), 1))
        dvr[pl.ds(16 * x, 16), :] = dv[x]

    for half in range(2):
        packed = jnp.zeros((16, 128), F32)
        for k in range(8):
            packed = jnp.where(lane16 // 16 == k, lane_roll(dv[8 * half + k], 16 * k + 8), packed)
        sdz[half] = packed
    for y in range(6):
        for j, first in enumerate((0, 10)):
            sdy[j, y] = dvr[pl.ds(first + y, 16, stride=16), :]
    for i, j, k, (a, b) in CORNER:
        x, y = (15 - a if i else a), (15 - b if j else b)
        sde[i, j, pl.ds(k, 1), :] = dvr[pl.ds(16 * x + y, 1), :]
    div_copies = []
    for dx, dy, dz in AROUND:
        here_x, here_y = (1 - dx) // 2, (1 - dy) // 2
        if dz == 0:
            if dy == 0:
                src, dst = dv.at[pl.ds(10 if dx > 0 else 0, 6)], rdx.at[here_x]
            elif dx == 0:
                src, dst = sdy.at[1 - here_y], rdy.at[here_y]
            else:
                src, dst = sde.at[1 - here_x, 1 - here_y], rde.at[here_x, here_y]
        else:
            half = pl.ds(0, 2) if dx == 0 else pl.ds(1 if dx > 0 else 0, 1)
            slot = pl.ds(1, 2) if dx == 0 else pl.ds(0 if dx > 0 else 3, 1)
            part = pl.ds(0, 16) if dy == 0 else pl.ds(8 if dy > 0 else 0, 8)
            rows = pl.ds(8, 16) if dy == 0 else pl.ds(0 if dy > 0 else 24, 8)
            src, dst = sdz.at[half, part, :], rdz.at[(1 - dz) // 2, slot, rows, :]
        div_copies.append(cp.start(src, dst, (dx, dy, dz)))

    for x in range(16):
        db[0, pl.ds(at0(x + 6) + 8, 16), :] = dv[x]
    for c in div_copies:
        c.wait_recv()
    for x in range(6):
        for side, p in ((0, x), (1, 22 + x)):
            db[0, pl.ds(at0(p) + 8, 16), :] = rdx[side, x]
    for i, j, k, (a, b) in CORNER:
        p, y = (22 + a if i else 5 - a), (16 + b if j else -1 - b)
        db[0, pl.ds(at0(p) + 8 + y, 1), :] = rde[i, j, pl.ds(k, 1), :]
    for y in range(6):
        db[0, pl.ds(at0(6) + 2 + y, 16, stride=32), :] = rdy[0, y]
        db[0, pl.ds(at0(6) + 24 + y, 16, stride=32), :] = rdy[1, y]
    lane32 = lanes((32, 128))
    for g in range(4):
        both = jnp.where(lane32 % 16 < 8, rdz[0, g], rdz[1, g])
        for k in range(8):
            x = 8 * (g - 1) + k
            if -6 <= x < 22:
                db[1, pl.ds(at0(x + 6), 32), :] = lane_roll(both, -(16 * k + 8))

    for p in range(1, 27, 2):
        b, around = sum6_wide(db, at0(p), 64, 32)
        for t in (0, 1):
            v0[t, pl.ds(at0(p), 64), :] = -C * (1.2 * b[t] + C * around[t])
    for k in range(12):
        for edge in (0, 24):
            rs[pl.ds(32 * k + edge, 8), :] = jnp.zeros((8, 256), F32)
        pair = [0.0, 0.0]
        for base in (at0(2 + 2 * k) + 4, at0(3 + 2 * k) + 4):
            v, around = sum6_wide(v0, base, 24, 32)
            for t in (0, 1):
                pair[t] = pair[t] + db[t, pl.ds(base, 24), :] - (around[t] - 6.0 * v[t])
        for t in (0, 1):
            rs[pl.ds(32 * k + 4, 24), pl.ds(128 * t, 128)] = pair[t]
    halve = jnp.where(coarse_lane((256, 128), 0) == lanes((256, 128)), 0.125, 0.0).astype(F32)
    rt[...] = exact_dot(rs[...], halve)
    s1[...] = rt[pl.ds(0, 192, stride=2), :] + rt[pl.ds(1, 192, stride=2), :]

    lane8 = lanes((8, 128))
    packed = jnp.zeros((8, 128), F32)
    for x in range(8):
        plane = s1[pl.ds(16 * (x + 2) + 4, 8), :]
        r1c[x] = plane
        packed = jnp.where(lane8 // 8 == 2 * x, lane_roll(plane, 16 * x - 88), packed)
        packed = jnp.where(lane8 // 8 == 2 * x + 1, lane_roll(plane, 16 * x + 8 - 32), packed)
    sez[...] = packed

    for p in range(1, 11, 5):
        b, around = sum6(s1, 16 * p, 80, 16)
        v1s[pl.ds(16 * p, 80), :] = -4.0 * C * (1.2 * b + C * around)
    parts = []
    for k in range(4):
        base = 16 * (2 + 2 * k)
        v, around = sum6(v1s, base, 32, 16)
        residual = s1[pl.ds(base, 32), :] - 0.25 * (around - 6.0 * v)
        parts.append(residual[0:16] + residual[16:32])
    halve = halve[0:128]
    rt[pl.ds(0, 64), :] = exact_dot(jnp.concatenate(parts, axis=0), halve)
    packed = jnp.zeros((8, 128), F32)
    for x in range(4):
        plane = rt[pl.ds(16 * x, 8, stride=2), :] + rt[pl.ds(16 * x + 1, 8, stride=2), :]
        packed = jnp.where(lane8 // 32 == x, lane_roll(plane, 32 * x - 48), packed)
    sa[...] = packed
    ra[3, 1] = packed
    yz_copies = [
        cp.start(sa, ra.at[3 - dy, 1 - dz], (0, dy, dz))
        for dy in (3, -3, 2, -2, 1, -1, 0)
        for dz in (1, -1, 0)
        if (dy, dz) != (0, 0)
    ]
    src_copies = []
    for dx, dy, dz in AROUND:
        here_x, here_y = (1 - dx) // 2, (1 - dy) // 2
        if dz == 0:
            planes = pl.ds(3 if dx > 0 else 0, 5)
            if dy == 0:
                src, dst = r1c.at[planes], rex.at[here_x]
            elif dx == 0:
                src, dst = r1c, rey.at[here_y]
            else:
                src, dst = r1c.at[planes], ree.at[here_x, here_y]
        else:
            src, dst = sez, rez.at[(1 - dz) // 2, 1 - dx, pl.ds(8 * (1 - dy), 8), :]
        src_copies.append(cp.start(src, dst, (dx, dy, dz)))

    for c in yz_copies:
        c.wait_recv()
    for dy in range(7):
        for x in range(4):
            before, here, after = (
                lane_roll(ra[dy, k], lane - 32 * x) for k, lane in ((0, 16), (1, 48), (2, 80))
            )
            whole = jnp.where(lane8 < 48, before, jnp.where(lane8 < 80, here, after))
            lb2[pl.ds(32 * (12 + x) + 4 * dy, 4), :] = whole[2:6]
    lane32 = lanes((32, 128))
    for k in range(2):
        left, right = lb2[pl.ds(32 * (12 + 2 * k), 32), :], lb2[pl.ds(32 * (13 + 2 * k), 32), :]
        sb[k] = jnp.where(lane32 < 64, lane_roll(left, -32), lane_roll(right, 32))
    x_copies = []
    for dx in (3, -3, 2, -2, 1, -1):
        rows = pl.ds(0, 24 if abs(dx) == 3 else 32)
        x_copies.append(cp.start(sb.at[:, rows, :], rb.at[3 - dx, :, rows, :], (dx, 0, 0)))

    for c in src_copies:
        c.wait_recv()
    lane24 = lanes((24, 128))
    for p in range(18):
        dx, x = (p - 5) // 8, (p - 5) % 8
        if dx == 0:
            three = [rey[0, x], r1c[x], rey[1, x]]
        else:
            side = (dx + 1) // 2
            k = x - 3 if dx < 0 else x
            three = [ree[side, 0, k], rex[side, k], ree[side, 1, k]]
        before = lane_roll(rez[0, dx + 1], 24 - 16 * x)
        after = lane_roll(rez[1, dx + 1], 96 - 16 * x - 8)
        here = jnp.concatenate(three, axis=0)
        lb1[pl.ds(24 * p, 24), :] = jnp.where(
            lane24 < 32, before, jnp.where(lane24 < 96, here, after)
        )
    for p in range(1, 17, 4):
        b, around = sum6(lb1, 24 * p, 96, 24)
        v1[pl.ds(24 * p, 96), :] = -4.0 * C * (1.2 * b + C * around)

    cp.sent()
    for c in x_copies:
        c.wait_recv()
    for dx in (-3, -2, -1, 1, 2, 3):
        n = 24 if abs(dx) == 3 else 32
        for x in range(4):
            plane = lane_roll(rb[3 + dx, x // 2, pl.ds(0, n), :], 32 if x % 2 == 0 else -32)
            lb2[pl.ds(32 * (4 * (3 + dx) + x), n), :] = plane

    for p in range(1, 27, 2):
        b, around = sum6(lb2, 32 * p, 64, 32)
        v2[pl.ds(32 * p, 64), :] = -16.0 * C * (1.2 * b + C * around)
    for k in range(12):
        base = 32 * (2 + 2 * k)
        v, around = sum6(v2, base, 64, 32)
        residual = lb2[pl.ds(base, 64), :] - 0.0625 * (around - 6.0 * v)
        rs[pl.ds(32 * k, 32), pl.ds(0, 128)] = residual[0:32] + residual[32:64]
    rt[...] = exact_dot(rs[:, 0:128], halve)
    lb3[...] = rt[pl.ds(0, 192, stride=2), :] + rt[pl.ds(1, 192, stride=2), :]

    b, around = sum6(lb3, 16, 160, 16)
    v3[pl.ds(16, 160), :] = -64.0 * C * (1.2 * b + C * around)
    v, around = sum6(v3, 32, 128, 16)
    u3[pl.ds(32, 128), :] = 0.2 * v + C * around - 64.0 * C * lb3[pl.ds(32, 128), :]
    v, around = sum6(u3, 48, 96, 16)
    coarse = 0.2 * v + C * around - 64.0 * C * lb3[pl.ds(48, 96), :]

    double = jnp.where(rows_of((128, 256)) == coarse_lane((128, 256), 1), 1.0, 0.0).astype(F32)
    fine = exact_dot(coarse, double[:, 0:128])
    for k in range(6):
        for p in (8 + 2 * k, 9 + 2 * k):
            for odd in (0, 1):
                where = pl.ds(32 * p + odd, 16, stride=2)
                v2[where, :] = v2[where, :] + fine[16 * k : 16 * k + 16]
    for p in range(9, 19, 2):
        v, around = sum6(v2, 32 * p, 64, 32)
        u2[pl.ds(32 * p, 64), :] = 0.2 * v + C * around - 16.0 * C * lb2[pl.ds(32 * p, 64), :]
    for k in range(4):
        base = 32 * (10 + 2 * k)
        v, around = sum6(u2, base, 64, 32)
        rs[pl.ds(64 * k, 64), pl.ds(0, 128)] = (
            0.2 * v + C * around - 16.0 * C * lb2[pl.ds(base, 64), :]
        )

    fine = exact_dot(rs[0:256, 0:128], double[:, 0:128])
    for k in range(8):
        for p in (1 + 2 * k, 2 + 2 * k):
            for odd in (0, 1):
                where = pl.ds(24 * p + odd, 12, stride=2)
                v1[where, :] = v1[where, :] + fine[32 * k + 8 : 32 * k + 20]
    for p in range(2, 16, 2):
        v, around = sum6(v1, 24 * p, 48, 24)
        u1[pl.ds(24 * p, 48), :] = 0.2 * v + C * around - 4.0 * C * lb1[pl.ds(24 * p, 48), :]
    for k in range(6):
        base = 24 * (3 + 2 * k)
        v, around = sum6(u1, base, 48, 24)
        rs[pl.ds(48 * k, 48), pl.ds(0, 128)] = (
            0.2 * v + C * around - 4.0 * C * lb1[pl.ds(base, 48), :]
        )

    for t in (0, 1):
        fine = exact_dot(rs[0:288, 0:128], double[:, 128 * t : 128 * t + 128])
        for k in range(12):
            for p in (2 + 2 * k, 3 + 2 * k):
                for odd in (0, 1):
                    where = pl.ds(at0(p) + odd, 16, stride=2)
                    v0[t, where, :] = v0[t, where, :] + fine[24 * k + 4 : 24 * k + 20]
    for p in range(4, 24):
        base = at0(p) + 4
        v, around = sum6_wide(v0, base, 24, 32)
        for t in (0, 1):
            b = db[t, pl.ds(base, 24), :]
            u0[t, pl.ds(base, 24), :] = 0.2 * v[t] + C * around[t] - C * b
    for p in range(5, 23):
        base = at0(p) + 4
        v, around = sum6_wide(u0, base, 24, 32)
        for t in (0, 1):
            b = db[t, pl.ds(base, 24), :]
            v0[t, pl.ds(base, 24), :] = 0.2 * v[t] + C * around[t] - C * b

    for x in range(16):
        base = at0(x + 6) + 8
        here, beyond = v0[0, pl.ds(base, 16), :], v0[1, pl.ds(base, 16), :]
        pout[x] = here
        slopes = [
            v0[0, pl.ds(base + 32, 16), :] - v0[0, pl.ds(base - 32, 16), :],
            v0[0, pl.ds(base + 1, 16), :] - v0[0, pl.ds(base - 1, 16), :],
            jnp.where(lane16 == 127, lane_roll(beyond, -1), lane_roll(here, -1))
            - jnp.where(lane16 == 0, lane_roll(beyond, 1), lane_roll(here, 1)),
        ]
        for c in range(3):
            vout[c, x] = pb[c, pl.ds(at(x), 16), :] - 0.5 * slopes[c]


def body(velocity, input_weight, input_bias, hidden_weight, hidden_bias, output_weight):
    def scratch(*shape):
        return pltpu.VMEM(shape, F32)

    plane_buffer = 16 + PLANE_ROWS * 20
    level0 = 16 + 32 * 28
    return pl.pallas_call(
        kernel,
        out_shape=(
            pltpu.VMEM((3, 16, 16, 128), F32),
            pltpu.VMEM((16, 16, 128), F32),
        ),
        in_specs=[pl.BlockSpec(memory_space=pltpu.HBM)] * 6,
        out_specs=[pl.BlockSpec(memory_space=pltpu.VMEM)] * 2,
        scratch_shapes=[
            scratch(3, 16, 16, 128),
            pltpu.VMEM((9, 32), BF16),
            scratch(1, 32),
            pltpu.VMEM((32, 32), BF16),
            scratch(1, 32),
            pltpu.VMEM((1, 32), BF16),
            pltpu.VMEM((256, 80), BF16),
            pltpu.VMEM((256, 256), BF16),
            pltpu.VMEM((16, 256), BF16),
            scratch(256, 128),
            scratch(256, 128),
            scratch(3, plane_buffer, 128),
            scratch(plane_buffer, 128),
            scratch(3, plane_buffer, 128),
            scratch(4, 3, 16, 128),
            scratch(3, 16, 128),
            scratch(2, 2, 8, 128),
            scratch(4, 3, 16, 128),
            scratch(2, 4, 32, 128),
            scratch(2, 2, 8, 128),
            scratch(2, 2, 4, 16, 128),
            scratch(4, 16, 128),
            scratch(16, 128),
            scratch(2, 2, 8, 128),
            scratch(4, 16, 128),
            scratch(2, 2, 8, 128),
            scratch(4, 32, 128),
            scratch(4, plane_buffer, 128),
            scratch(16, 16, 128),
            scratch(256, 128),
            scratch(2, 6, 16, 128),
            scratch(2, 2, 16, 128),
            scratch(2, 16, 128),
            scratch(2, 6, 16, 128),
            scratch(2, 6, 16, 128),
            scratch(2, 2, 16, 128),
            scratch(2, 4, 32, 128),
            scratch(2, level0, 128),
            scratch(2, level0, 128),
            scratch(2, level0, 128),
            scratch(384, 256),
            scratch(384, 128),
            scratch(192, 128),
            scratch(192, 128),
            scratch(8, 8, 128),
            scratch(8, 128),
            scratch(2, 5, 8, 128),
            scratch(2, 8, 8, 128),
            scratch(2, 2, 5, 8, 128),
            scratch(2, 3, 24, 128),
            scratch(432, 128),
            scratch(432, 128),
            scratch(432, 128),
            scratch(8, 128),
            scratch(7, 3, 8, 128),
            scratch(2, 32, 128),
            scratch(7, 2, 32, 128),
            scratch(896, 128),
            scratch(896, 128),
            scratch(896, 128),
            scratch(192, 128),
            scratch(192, 128),
            scratch(192, 128),
            pltpu.SemaphoreType.DMA((N_COPIES,)),
            pltpu.SemaphoreType.DMA((N_COPIES,)),
            pltpu.SemaphoreType.DMA((6,)),
        ],
        compiler_params=pltpu.CompilerParams(
            collective_id=0, has_side_effects=True, vmem_limit_bytes=60 * 1024 * 1024
        ),
    )(
        velocity,
        input_weight.T,
        input_bias.reshape(1, 32),
        hidden_weight,
        hidden_bias.reshape(1, 32),
        output_weight.reshape(1, 32),
    )


def solution(mesh):
    return jax.shard_map(
        body,
        mesh=mesh,
        in_specs=(P(None, "gx", "gy", "gz"), P(), P(), P(), P(), P()),
        out_specs=(P(None, "gx", "gy", "gz"), P("gx", "gy", "gz")),
        check_vma=False,
    )
```

```python
import jax
import jax.numpy as jnp
from jax import lax
from jax.experimental import pallas as pl
from jax.experimental.pallas import tpu as pltpu
from jax.sharding import PartitionSpec as P

MESH = pl.DeviceIdType.MESH
AXES = ("gx", "gy", "gz")
F32, BF16 = jnp.float32, jnp.bfloat16

TIME_STEP = 0.1
GAIN = 0.5
C = 0.8 / 6.0

FACES = [(1, 0, 0), (-1, 0, 0), (0, 1, 0), (0, -1, 0), (0, 0, 1), (0, 0, -1)]
AROUND = [
    (i, j, k) for i in (-1, 0, 1) for j in (-1, 0, 1) for k in (-1, 0, 1) if (i, j, k) != (0, 0, 0)
]
PLANE_ROWS = 24
NEAR = [(a, b) for a in range(5) for b in range(5) if a + b <= 4]
CORNER = [(i, j, k, o) for i in (0, 1) for j in (0, 1) for k, o in enumerate(NEAR)]
EDGES = [o for o in AROUND if abs(o[0]) + abs(o[1]) + abs(o[2]) == 2]
N_COPIES = 6 + 16 + 20 + 26 * 2 + 20 + 6


def at(x, y=0):
    return 8 + PLANE_ROWS * (x + 2) + y


def column(y):
    return pl.ds(at(0, y), 16, stride=PLANE_ROWS)


def at0(p):
    return 8 + 32 * p


def lanes(shape):
    return lax.broadcasted_iota(jnp.int32, shape, len(shape) - 1)


def rows_of(shape):
    return lax.broadcasted_iota(jnp.int32, shape, len(shape) - 2)


def lane_roll(value, shift):
    return pltpu.roll(value, shift % 128, value.ndim - 1)


def dot(a, b, precision=None):
    return jnp.dot(a, b, precision=precision, preferred_element_type=F32)


def coarse_lane(shape, axis):
    fine = lax.broadcasted_iota(jnp.int32, shape, axis)
    return jnp.where(fine < 192, 32 + fine // 2, fine // 2 - 96)


def exact_dot(a, b):
    b = b.astype(BF16)
    first = a.astype(BF16)
    rest = a - first.astype(F32)
    second = rest.astype(BF16)
    third = (rest - second.astype(F32)).astype(BF16)
    return dot(third, b) + dot(second, b) + dot(first, b)


class Copies:
    def __init__(self, ids, send_sem, recv_sem):
        self.ids, self.send_sem, self.recv_sem = ids, send_sem, recv_sem
        self.made, self.count = [], 0

    def device(self, offset):
        return tuple(lax.rem(i + 8 + o, 8) for i, o in zip(self.ids, offset))

    def start(self, src, dst, offset):
        k = self.count + len(self.made)
        copy = pltpu.make_async_remote_copy(
            src_ref=src,
            dst_ref=dst,
            send_sem=self.send_sem.at[k],
            recv_sem=self.recv_sem.at[k],
            device_id=self.device(offset),
            device_id_type=MESH,
        )
        copy.start()
        self.made.append(copy)
        return copy

    def sent(self):
        for copy in self.made:
            copy.wait_send()
        self.count += len(self.made)
        self.made = []


def sum6(ref, base, n, period):
    center = ref[pl.ds(base, n), :]
    total = ref[pl.ds(base + period, n), :] + ref[pl.ds(base - period, n), :]
    total = total + ref[pl.ds(base + 1, n), :] + ref[pl.ds(base - 1, n), :]
    return center, total + lane_roll(center, 1) + lane_roll(center, -1)


def sum6_wide(ref, base, n, period):
    center = [ref[t, pl.ds(base, n), :] for t in (0, 1)]
    lane = lanes((n, 128))
    up = [lane_roll(c, -1) for c in center]
    down = [lane_roll(c, 1) for c in center]
    out = []
    for t in (0, 1):
        total = ref[t, pl.ds(base + period, n), :] + ref[t, pl.ds(base - period, n), :]
        total = total + ref[t, pl.ds(base + 1, n), :] + ref[t, pl.ds(base - 1, n), :]
        total = total + jnp.where(lane == 127, up[1 - t], up[t])
        out.append(total + jnp.where(lane == 0, down[1 - t], down[t]))
    return center, out


def kernel(
    vel_in, w1_in, b1_in, w2_in, b2_in, w3_in, vout, pout,
    vel, w1, b1, w2, b2, w3, w1k, w2k, w3k, b1k, b2k,
    vb, nb, pb, sy, sz, sxy, ry, rz, rxy, rxz, syn, szn, sxyn, ryn, rxyn, cz, zb,
    dv, dvr, sdy, sde, sdz, rdx, rdy, rde, rdz, db, v0, u0,
    rs, rt, s1, v1s, r1c, sez, rex, rey, ree, rez, lb1, v1, u1,
    sa, ra, sb, rb, lb2, v2, u2, lb3, v3, u3,
    send_sem, recv_sem, load_sem,
):
    ids = [lax.axis_index(a) for a in AXES]
    cp = Copies(ids, send_sem, recv_sem)
    barrier = pltpu.get_barrier_semaphore()
    for offset in FACES:
        pl.semaphore_signal(barrier, inc=1, device_id=cp.device(offset), device_id_type=MESH)

    loads = [
        pltpu.make_async_copy(src, dst, load_sem.at[k])
        for k, (src, dst) in enumerate(
            ((vel_in, vel), (w1_in, w1), (b1_in, b1), (w2_in, w2), (b2_in, b2), (w3_in, w3))
        )
    ]
    for load in loads:
        load.start()
    loads[0].wait()
    for c in range(3):
        for x in range(16):
            vb[c, pl.ds(at(x), 16), :] = vel[c, x]

    lane16 = lanes((16, 128))

    def pack_z(plane_of):
        packed = jnp.zeros((16, 128), F32)
        for x in range(16):
            plane = plane_of(x)
            packed = jnp.where(lane16 // 2 == 4 * x + 1, lane_roll(plane, 8 * x + 2), packed)
            packed = jnp.where(lane16 // 2 == 4 * x + 2, lane_roll(plane, 8 * x + 6), packed)
        return packed

    for c in range(3):
        for k, y in enumerate((0, 1, 14, 15)):
            sy[k, c] = vb[c, column(y), :]
        sz[c] = pack_z(lambda x: vel[c, x])
        for i in (0, 1):
            for j in (0, 1):
                sxy[i, j, pl.ds(c, 1), :] = vel[c, 15 * i, pl.ds(15 * j, 1), :]

    pl.semaphore_wait(barrier, len(FACES))

    vel_copies = [
        cp.start(sz, rz.at[0, pl.ds(0, 3), pl.ds(8, 16), :], (0, 0, 1)),
        cp.start(sz, rz.at[1, pl.ds(0, 3), pl.ds(8, 16), :], (0, 0, -1)),
        cp.start(sy.at[3], ry.at[1], (0, 1, 0)),
        cp.start(sy.at[0], ry.at[2], (0, -1, 0)),
        cp.start(vel.at[:, 15], vb.at[:, pl.ds(at(-1), 16), :], (1, 0, 0)),
        cp.start(vel.at[:, 0], vb.at[:, pl.ds(at(16), 16), :], (-1, 0, 0)),
    ]

    for load in loads[1:]:
        load.wait()
    spread = (rows_of((256, 32)) // 8 == lanes((256, 32))).astype(BF16)
    spread_t = (rows_of((32, 256)) == lanes((32, 256)) // 8).astype(BF16)
    columns = (rows_of((80, 9)) // 8 == lanes((80, 9))).astype(BF16)
    wide = lax.dot_general(
        spread, dot(columns, w1[...]).astype(BF16), (((1,), (1,)), ((), ())), preferred_element_type=F32
    )
    same = rows_of((256, 80)) % 8 == lanes((256, 80)) % 8
    w1k[...] = jnp.where(same, wide, 0.0).astype(BF16)
    wide = dot(dot(spread, w2[...]).astype(BF16), spread_t)
    same = rows_of((256, 256)) % 8 == lanes((256, 256)) % 8
    w2k[...] = jnp.where(same, wide, 0.0).astype(BF16)
    wide = jnp.broadcast_to(dot(w3[...], spread_t), (16, 256))
    same = rows_of((16, 256)) == lanes((16, 256)) % 8
    w3k[...] = jnp.where(same, wide, 0.0).astype(BF16)
    mine = rows_of((256, 32)) // 8 == lanes((256, 32))
    for bias, kept in ((b1, b1k), (b2, b2k)):
        bias_column = jnp.sum(jnp.where(mine, bias[...], 0.0), axis=1, keepdims=True)
        kept[...] = jnp.broadcast_to(bias_column, (256, 128))
    lb2[...] = jnp.zeros_like(lb2)
    for p in range(28):
        for first in (0, 24):
            db[0, pl.ds(at0(p) + first, 8), :] = jnp.zeros((8, 128), F32)
    for c in vel_copies:
        c.wait_recv()
    for c in range(3):
        vb[c, column(-1), :] = ry[1, c]
        vb[c, column(16), :] = ry[2, c]

    for first_x in range(0, 16, 8):
        listing = [[] for _ in range(10)]
        for x in range(first_x, first_x + 8):
            base = at(x)
            g = []
            for c in range(3):
                plane = vb[c, pl.ds(base, 16), :]
                after = lane_roll(rz[1, c, pl.ds(8, 16), :], 125 - 8 * x)
                before = lane_roll(rz[0, c, pl.ds(8, 16), :], -(8 * x + 5))
                after = jnp.where(lane16 == 127, after, lane_roll(plane, -1))
                before = jnp.where(lane16 == 0, before, lane_roll(plane, 1))
                around = [
                    (vb[c, pl.ds(base + step, 16), :], vb[c, pl.ds(base - step, 16), :])
                    for step in (PLANE_ROWS, 1)
                ]
                g.append([0.5 * (a - b) for a, b in around + [(after, before)]])
            entries = [
                g[0][0], g[1][1], g[2][2],
                0.5 * (g[0][1] + g[1][0]), 0.5 * (g[0][2] + g[2][0]), 0.5 * (g[1][2] + g[2][1]),
                0.5 * (g[0][1] - g[1][0]), 0.5 * (g[0][2] - g[2][0]), 0.5 * (g[1][2] - g[2][1]),
                jnp.zeros((16, 128), F32),
            ]
            for tiles, entry in zip(listing, entries):
                tiles += [entry[0:8], entry[8:16]]
        features = jnp.concatenate(
            [jnp.concatenate(tiles, axis=1) for tiles in listing], axis=0
        ).astype(BF16)
        if first_x == 0:
            more_copies = []
            for dx, dy, dz in EDGES:
                i, j, k = (1 - dx) // 2, (1 - dy) // 2, (1 - dz) // 2
                if dz == 0:
                    src, dst = sxy.at[1 - i, 1 - j], rxy.at[i, j]
                elif dy == 0:
                    src, dst = sz, rxz.at[k, i, pl.ds(0, 3)]
                else:
                    part, rows = pl.ds(8 * (1 - j), 8), pl.ds(24 * j, 8)
                    src, dst = sz.at[:, part, :], rz.at[k, pl.ds(0, 3), rows, :]
                more_copies.append(cp.start(src, dst, (dx, dy, dz)))
            more_copies += [
                cp.start(sy.at[2], ry.at[0], (0, 1, 0)),
                cp.start(sy.at[1], ry.at[3], (0, -1, 0)),
                cp.start(vel.at[:, 14], vb.at[:, pl.ds(at(-2), 16), :], (1, 0, 0)),
                cp.start(vel.at[:, 1], vb.at[:, pl.ds(at(17), 16), :], (-1, 0, 0)),
            ]
        bias = jnp.concatenate([b1k[...]] * 16, axis=1)
        hidden = jnp.tanh(dot(w1k[...], features) + bias).astype(BF16)
        bias = jnp.concatenate([b2k[...]] * 16, axis=1)
        second = jnp.tanh(dot(w2k[...], hidden) + bias).astype(BF16)
        s = dot(w3k[...], second)[0:8]
        soft = GAIN * (jnp.maximum(s, 0.0) + jnp.log1p(jnp.exp(-jnp.abs(s))))
        for k in range(16):
            nb[pl.ds(at(first_x + k // 2, 8 * (k % 2)), 8), :] = soft[:, 128 * k : 128 * k + 128]

    for k, y in enumerate((0, 1, 14, 15)):
        syn[k] = nb[column(y), :]
    szn[...] = pack_z(lambda x: nb[pl.ds(at(x), 16), :])
    for i in (0, 1):
        for j in (0, 1):
            sxyn[i, j, pl.ds(0, 1), :] = nb[pl.ds(at(15 * i, 15 * j), 1), :]
    visc_copies = []
    for dx, dy, dz in EDGES:
        i, j, k = (1 - dx) // 2, (1 - dy) // 2, (1 - dz) // 2
        if dz == 0:
            src, dst = sxyn.at[1 - i, 1 - j], rxyn.at[i, j]
        elif dy == 0:
            src, dst = szn, rxz.at[k, i, 3]
        else:
            part, rows = pl.ds(8 * (1 - j), 8), pl.ds(24 * j, 8)
            src, dst = szn.at[part, :], rz.at[k, 3, rows, :]
        visc_copies.append(cp.start(src, dst, (dx, dy, dz)))
    visc_copies += [
        cp.start(szn, rz.at[0, 3, pl.ds(8, 16), :], (0, 0, 1)),
        cp.start(szn, rz.at[1, 3, pl.ds(8, 16), :], (0, 0, -1)),
        cp.start(syn.at[pl.ds(2, 2)], ryn.at[pl.ds(0, 2)], (0, 1, 0)),
        cp.start(syn.at[pl.ds(0, 2)], ryn.at[pl.ds(2, 2)], (0, -1, 0)),
    ]
    for x in (14, 15):
        here, there = pl.ds(at(x), 16), pl.ds(at(x - 16), 16)
        visc_copies.append(cp.start(nb.at[here, :], nb.at[there, :], (1, 0, 0)))
    for x in (0, 1):
        here, there = pl.ds(at(x), 16), pl.ds(at(x + 16), 16)
        visc_copies.append(cp.start(nb.at[here, :], nb.at[there, :], (-1, 0, 0)))

    slot = lanes((32, 128)) % 8

    def beyond(f, own):
        none = jnp.zeros((8, 128), F32)
        whole = jnp.concatenate([none, own, none], axis=0)
        outer = jnp.where(slot < 4, lane_roll(rz[0, f], -4), lane_roll(rz[1, f], 4))
        whole = jnp.where((slot >= 2) & (slot < 6), whole, outer)
        cz[f] = whole
        ends = jnp.where(slot == 0, lane_roll(whole, -1), lane_roll(whole, -5))
        for x in range(16):
            zb[f, pl.ds(at(x, -4), 24), :] = lane_roll(ends, -(8 * x + 1))[4:28]
        zb[f, pl.ds(at(-1), 16), :] = jnp.where(
            lane16 == 127, lane_roll(rxz[0, 0, f], 2), lane_roll(rxz[1, 0, f], 6)
        )
        zb[f, pl.ds(at(16), 16), :] = jnp.where(
            lane16 == 127, lane_roll(rxz[0, 1, f], 122), lane_roll(rxz[1, 1, f], -2)
        )

    for c in more_copies:
        c.wait_recv()
    for c in range(3):
        vb[c, column(-2), :] = ry[0, c]
        vb[c, column(17), :] = ry[3, c]
        for i in (0, 1):
            for j in (0, 1):
                vb[c, pl.ds(at(17 * i - 1, 17 * j - 1), 1), :] = rxy[i, j, pl.ds(c, 1), :]
        beyond(c, sz[c])
    for c in visc_copies:
        c.wait_recv()
    for k, y in enumerate((-2, -1, 16, 17)):
        nb[column(y), :] = ryn[k]
    for i in (0, 1):
        for j in (0, 1):
            nb[pl.ds(at(17 * i - 1, 17 * j - 1), 1), :] = rxyn[i, j, pl.ds(0, 1), :]
    beyond(3, szn[...])

    def change(i, n_mid, n_near, v_mid, v_near):
        total = 0.0
        for j in range(3):
            (up, down), (up_j, down_j) = v_near[i][j], v_near[j][j]
            total = total + 0.5 * (n_mid + n_near[j][0]) * (up - v_mid[i])
            total = total - 0.5 * (n_mid + n_near[j][1]) * (v_mid[i] - down)
            total = total - 0.5 * (up_j * up - down_j * down)
        return v_mid[i] + TIME_STEP * total

    def near(load, ends, start, n):
        mid = load(start)
        lane = lanes((n, 128))
        return mid, [
            (load(start + PLANE_ROWS), load(start - PLANE_ROWS)),
            (load(start + 1), load(start - 1)),
            (
                lane_roll(jnp.where(lane == 0, ends, mid), -1),
                lane_roll(jnp.where(lane == 127, ends, mid), 1),
            ),
        ]

    def tendency(start, n, components):
        where = pl.ds(start, n)
        n_mid, n_near = near(lambda r: nb[pl.ds(r, n), :], zb[3, where, :], start, n)
        both = [near(lambda r, c=c: vb[c, pl.ds(r, n), :], zb[c, where, :], start, n) for c in range(3)]
        for i in components:
            pb[i, where, :] = change(i, n_mid, n_near, [b[0] for b in both], [b[1] for b in both])

    for x in range(16):
        tendency(at(x), 16, (0, 1, 2))
    tendency(at(-1), 16, (0,))
    tendency(at(16), 16, (0,))
    for x in range(-1, 16):
        tendency(at(x, 16), 8, (1,))

    def near_end(f):
        mid = cz[f, pl.ds(8, 16), :]
        above = jnp.where(lane16 == 126, lane_roll(rxz[1, 1, f], 124), lane_roll(rxz[0, 1, f], 116))
        below = jnp.where(lane16 == 6, lane_roll(rxz[1, 0, f], 12), lane_roll(rxz[0, 0, f], 4))
        return mid, [
            (
                jnp.where(lane16 >= 120, above, lane_roll(mid, -8)),
                jnp.where(lane16 < 8, below, lane_roll(mid, 8)),
            ),
            (cz[f, pl.ds(9, 16), :], cz[f, pl.ds(7, 16), :]),
            (lane_roll(mid, -1), lane_roll(mid, 1)),
        ]

    fields = [near_end(f) for f in range(4)]
    far = change(2, *fields[3], [f[0] for f in fields[:3]], [f[1] for f in fields[:3]])
    far = jnp.where(lane16 % 8 == 0, lane_roll(far, -1), lane_roll(far, -5))

    for x in range(16):
        base = at(x)
        plane, ends = pb[2, pl.ds(base, 16), :], lane_roll(far, -(8 * x + 1))
        total = pb[0, pl.ds(base + PLANE_ROWS, 16), :] - pb[0, pl.ds(base - PLANE_ROWS, 16), :]
        total = total + pb[1, pl.ds(base + 1, 16), :] - pb[1, pl.ds(base - 1, 16), :]
        total = total + lane_roll(jnp.where(lane16 == 0, ends, plane), -1)
        dv[x] = 0.5 * (total - lane_roll(jnp.where(lane16 == 127, ends, plane), 1))
        dvr[pl.ds(16 * x, 16), :] = dv[x]

    for half in range(2):
        packed = jnp.zeros((16, 128), F32)
        for k in range(8):
            packed = jnp.where(lane16 // 16 == k, lane_roll(dv[8 * half + k], 16 * k + 8), packed)
        sdz[half] = packed
    for y in range(6):
        for j, first in enumerate((0, 10)):
            sdy[j, y] = dvr[pl.ds(first + y, 16, stride=16), :]
    for i, j, k, (a, b) in CORNER:
        x, y = (15 - a if i else a), (15 - b if j else b)
        sde[i, j, pl.ds(k, 1), :] = dvr[pl.ds(16 * x + y, 1), :]
    div_copies = []
    for dx, dy, dz in AROUND:
        here_x, here_y = (1 - dx) // 2, (1 - dy) // 2
        if dz == 0:
            if dy == 0:
                src, dst = dv.at[pl.ds(10 if dx > 0 else 0, 6)], rdx.at[here_x]
            elif dx == 0:
                src, dst = sdy.at[1 - here_y], rdy.at[here_y]
            else:
                src, dst = sde.at[1 - here_x, 1 - here_y], rde.at[here_x, here_y]
        else:
            half = pl.ds(0, 2) if dx == 0 else pl.ds(1 if dx > 0 else 0, 1)
            slot = pl.ds(1, 2) if dx == 0 else pl.ds(0 if dx > 0 else 3, 1)
            part = pl.ds(0, 16) if dy == 0 else pl.ds(8 if dy > 0 else 0, 8)
            rows = pl.ds(8, 16) if dy == 0 else pl.ds(0 if dy > 0 else 24, 8)
            src, dst = sdz.at[half, part, :], rdz.at[(1 - dz) // 2, slot, rows, :]
        div_copies.append(cp.start(src, dst, (dx, dy, dz)))

    for x in range(16):
        db[0, pl.ds(at0(x + 6) + 8, 16), :] = dv[x]
    for c in div_copies:
        c.wait_recv()
    for x in range(6):
        for side, p in ((0, x), (1, 22 + x)):
            db[0, pl.ds(at0(p) + 8, 16), :] = rdx[side, x]
    for i, j, k, (a, b) in CORNER:
        p, y = (22 + a if i else 5 - a), (16 + b if j else -1 - b)
        db[0, pl.ds(at0(p) + 8 + y, 1), :] = rde[i, j, pl.ds(k, 1), :]
    for y in range(6):
        db[0, pl.ds(at0(6) + 2 + y, 16, stride=32), :] = rdy[0, y]
        db[0, pl.ds(at0(6) + 24 + y, 16, stride=32), :] = rdy[1, y]
    lane32 = lanes((32, 128))
    for g in range(4):
        both = jnp.where(lane32 % 16 < 8, rdz[0, g], rdz[1, g])
        for k in range(8):
            x = 8 * (g - 1) + k
            if -6 <= x < 22:
                db[1, pl.ds(at0(x + 6), 32), :] = lane_roll(both, -(16 * k + 8))

    for p in range(1, 27, 2):
        b, around = sum6_wide(db, at0(p), 64, 32)
        for t in (0, 1):
            v0[t, pl.ds(at0(p), 64), :] = -C * (1.2 * b[t] + C * around[t])
    for k in range(12):
        for edge in (0, 24):
            rs[pl.ds(32 * k + edge, 8), :] = jnp.zeros((8, 256), F32)
        pair = [0.0, 0.0]
        for base in (at0(2 + 2 * k) + 4, at0(3 + 2 * k) + 4):
            v, around = sum6_wide(v0, base, 24, 32)
            for t in (0, 1):
                pair[t] = pair[t] + db[t, pl.ds(base, 24), :] - (around[t] - 6.0 * v[t])
        for t in (0, 1):
            rs[pl.ds(32 * k + 4, 24), pl.ds(128 * t, 128)] = pair[t]
    halve = jnp.where(coarse_lane((256, 128), 0) == lanes((256, 128)), 0.125, 0.0).astype(F32)
    rt[...] = exact_dot(rs[...], halve)
    s1[...] = rt[pl.ds(0, 192, stride=2), :] + rt[pl.ds(1, 192, stride=2), :]

    lane8 = lanes((8, 128))
    packed = jnp.zeros((8, 128), F32)
    for x in range(8):
        plane = s1[pl.ds(16 * (x + 2) + 4, 8), :]
        r1c[x] = plane
        packed = jnp.where(lane8 // 8 == 2 * x, lane_roll(plane, 16 * x - 88), packed)
        packed = jnp.where(lane8 // 8 == 2 * x + 1, lane_roll(plane, 16 * x + 8 - 32), packed)
    sez[...] = packed

    for p in range(1, 11, 5):
        b, around = sum6(s1, 16 * p, 80, 16)
        v1s[pl.ds(16 * p, 80), :] = -4.0 * C * (1.2 * b + C * around)
    parts = []
    for k in range(4):
        base = 16 * (2 + 2 * k)
        v, around = sum6(v1s, base, 32, 16)
        residual = s1[pl.ds(base, 32), :] - 0.25 * (around - 6.0 * v)
        parts.append(residual[0:16] + residual[16:32])
    halve = halve[0:128]
    rt[pl.ds(0, 64), :] = exact_dot(jnp.concatenate(parts, axis=0), halve)
    packed = jnp.zeros((8, 128), F32)
    for x in range(4):
        plane = rt[pl.ds(16 * x, 8, stride=2), :] + rt[pl.ds(16 * x + 1, 8, stride=2), :]
        packed = jnp.where(lane8 // 32 == x, lane_roll(plane, 32 * x - 48), packed)
    sa[...] = packed[2:6]
    ra[3, 1] = packed[2:6]
    yz_copies = [
        cp.start(sa, ra.at[3 - dy, 1 - dz], (0, dy, dz))
        for dy in (3, -3, 2, -2, 1, -1, 0)
        for dz in (1, -1, 0)
        if (dy, dz) != (0, 0)
    ]
    src_copies = []
    for dx, dy, dz in AROUND:
        here_x, here_y = (1 - dx) // 2, (1 - dy) // 2
        if dz == 0:
            planes = pl.ds(3 if dx > 0 else 0, 5)
            if dy == 0:
                src, dst = r1c.at[planes], rex.at[here_x]
            elif dx == 0:
                src, dst = r1c, rey.at[here_y]
            else:
                src, dst = r1c.at[planes], ree.at[here_x, here_y]
        else:
            src, dst = sez, rez.at[(1 - dz) // 2, 1 - dx, pl.ds(8 * (1 - dy), 8), :]
        src_copies.append(cp.start(src, dst, (dx, dy, dz)))

    for c in yz_copies:
        c.wait_recv()
    lane4 = lanes((4, 128))
    for dy in range(7):
        for x in range(4):
            before, here, after = (
                lane_roll(ra[dy, k], lane - 32 * x) for k, lane in ((0, 16), (1, 48), (2, 80))
            )
            whole = jnp.where(lane4 < 48, before, jnp.where(lane4 < 80, here, after))
            lb2[pl.ds(32 * (12 + x) + 4 * dy, 4), :] = whole
    lane32 = lanes((32, 128))
    for k in range(2):
        left, right = lb2[pl.ds(32 * (12 + 2 * k), 32), :], lb2[pl.ds(32 * (13 + 2 * k), 32), :]
        sb[k] = jnp.where(lane32 < 64, lane_roll(left, -32), lane_roll(right, 32))
    x_copies = []
    for dx in (3, -3, 2, -2, 1, -1):
        rows = pl.ds(0, 24 if abs(dx) == 3 else 32)
        x_copies.append(cp.start(sb.at[:, rows, :], rb.at[3 - dx, :, rows, :], (dx, 0, 0)))

    for c in src_copies:
        c.wait_recv()
    lane24 = lanes((24, 128))
    for p in range(18):
        dx, x = (p - 5) // 8, (p - 5) % 8
        if dx == 0:
            three = [rey[0, x], r1c[x], rey[1, x]]
        else:
            side = (dx + 1) // 2
            k = x - 3 if dx < 0 else x
            three = [ree[side, 0, k], rex[side, k], ree[side, 1, k]]
        before = lane_roll(rez[0, dx + 1], 24 - 16 * x)
        after = lane_roll(rez[1, dx + 1], 96 - 16 * x - 8)
        here = jnp.concatenate(three, axis=0)
        lb1[pl.ds(24 * p, 24), :] = jnp.where(
            lane24 < 32, before, jnp.where(lane24 < 96, here, after)
        )
    for p in range(1, 17, 4):
        b, around = sum6(lb1, 24 * p, 96, 24)
        v1[pl.ds(24 * p, 96), :] = -4.0 * C * (1.2 * b + C * around)

    cp.sent()
    for c in x_copies:
        c.wait_recv()
    for dx in (-3, -2, -1, 1, 2, 3):
        n = 24 if abs(dx) == 3 else 32
        for x in range(4):
            plane = lane_roll(rb[3 + dx, x // 2, pl.ds(0, n), :], 32 if x % 2 == 0 else -32)
            lb2[pl.ds(32 * (4 * (3 + dx) + x), n), :] = plane

    for p in range(1, 27, 2):
        b, around = sum6(lb2, 32 * p, 64, 32)
        v2[pl.ds(32 * p, 64), :] = -16.0 * C * (1.2 * b + C * around)
    for k in range(12):
        base = 32 * (2 + 2 * k)
        v, around = sum6(v2, base, 64, 32)
        residual = lb2[pl.ds(base, 64), :] - 0.0625 * (around - 6.0 * v)
        rs[pl.ds(32 * k, 32), pl.ds(0, 128)] = residual[0:32] + residual[32:64]
    rt[...] = exact_dot(rs[:, 0:128], halve)
    lb3[...] = rt[pl.ds(0, 192, stride=2), :] + rt[pl.ds(1, 192, stride=2), :]

    b, around = sum6(lb3, 16, 160, 16)
    v3[pl.ds(16, 160), :] = -64.0 * C * (1.2 * b + C * around)
    v, around = sum6(v3, 32, 128, 16)
    u3[pl.ds(32, 128), :] = 0.2 * v + C * around - 64.0 * C * lb3[pl.ds(32, 128), :]
    v, around = sum6(u3, 48, 96, 16)
    coarse = 0.2 * v + C * around - 64.0 * C * lb3[pl.ds(48, 96), :]

    double = jnp.where(rows_of((128, 256)) == coarse_lane((128, 256), 1), 1.0, 0.0).astype(F32)
    fine = exact_dot(coarse, double[:, 0:128])
    for k in range(6):
        for p in (8 + 2 * k, 9 + 2 * k):
            for odd in (0, 1):
                where = pl.ds(32 * p + odd, 16, stride=2)
                v2[where, :] = v2[where, :] + fine[16 * k : 16 * k + 16]
    for p in range(9, 19, 2):
        v, around = sum6(v2, 32 * p, 64, 32)
        u2[pl.ds(32 * p, 64), :] = 0.2 * v + C * around - 16.0 * C * lb2[pl.ds(32 * p, 64), :]
    for k in range(4):
        base = 32 * (10 + 2 * k)
        v, around = sum6(u2, base, 64, 32)
        rs[pl.ds(64 * k, 64), pl.ds(0, 128)] = (
            0.2 * v + C * around - 16.0 * C * lb2[pl.ds(base, 64), :]
        )

    fine = exact_dot(rs[0:256, 0:128], double[:, 0:128])
    for k in range(8):
        for p in (1 + 2 * k, 2 + 2 * k):
            for odd in (0, 1):
                where = pl.ds(24 * p + odd, 12, stride=2)
                v1[where, :] = v1[where, :] + fine[32 * k + 8 : 32 * k + 20]
    for p in range(2, 16, 2):
        v, around = sum6(v1, 24 * p, 48, 24)
        u1[pl.ds(24 * p, 48), :] = 0.2 * v + C * around - 4.0 * C * lb1[pl.ds(24 * p, 48), :]
    for k in range(6):
        base = 24 * (3 + 2 * k)
        v, around = sum6(u1, base, 48, 24)
        rs[pl.ds(48 * k, 48), pl.ds(0, 128)] = (
            0.2 * v + C * around - 4.0 * C * lb1[pl.ds(base, 48), :]
        )

    for t in (0, 1):
        fine = exact_dot(rs[0:288, 0:128], double[:, 128 * t : 128 * t + 128])
        for k in range(12):
            for p in (2 + 2 * k, 3 + 2 * k):
                for odd in (0, 1):
                    where = pl.ds(at0(p) + odd, 16, stride=2)
                    v0[t, where, :] = v0[t, where, :] + fine[24 * k + 4 : 24 * k + 20]
    for p in range(4, 24):
        base = at0(p) + 4
        v, around = sum6_wide(v0, base, 24, 32)
        for t in (0, 1):
            b = db[t, pl.ds(base, 24), :]
            u0[t, pl.ds(base, 24), :] = 0.2 * v[t] + C * around[t] - C * b
    for p in range(5, 23):
        base = at0(p) + 4
        v, around = sum6_wide(u0, base, 24, 32)
        for t in (0, 1):
            b = db[t, pl.ds(base, 24), :]
            v0[t, pl.ds(base, 24), :] = 0.2 * v[t] + C * around[t] - C * b

    for x in range(16):
        base = at0(x + 6) + 8
        here, beyond = v0[0, pl.ds(base, 16), :], v0[1, pl.ds(base, 16), :]
        pout[x] = here
        slopes = [
            v0[0, pl.ds(base + 32, 16), :] - v0[0, pl.ds(base - 32, 16), :],
            v0[0, pl.ds(base + 1, 16), :] - v0[0, pl.ds(base - 1, 16), :],
            jnp.where(lane16 == 127, lane_roll(beyond, -1), lane_roll(here, -1))
            - jnp.where(lane16 == 0, lane_roll(beyond, 1), lane_roll(here, 1)),
        ]
        for c in range(3):
            vout[c, x] = pb[c, pl.ds(at(x), 16), :] - 0.5 * slopes[c]


def hand_over(velocity, pressure, velocity_out, pressure_out, sem):
    first = pltpu.make_async_copy(velocity, velocity_out, sem.at[0])
    second = pltpu.make_async_copy(pressure, pressure_out, sem.at[1])
    first.start()
    second.start()
    first.wait()
    second.wait()


def body(velocity, input_weight, input_bias, hidden_weight, hidden_bias, output_weight):
    def scratch(*shape):
        return pltpu.VMEM(shape, F32)

    plane_buffer = 16 + PLANE_ROWS * 20
    level0 = 16 + 32 * 28
    results = pl.pallas_call(
        kernel,
        out_shape=(
            pltpu.VMEM((3, 16, 16, 128), F32),
            pltpu.VMEM((16, 16, 128), F32),
        ),
        in_specs=[pl.BlockSpec(memory_space=pltpu.HBM)] * 6,
        out_specs=[pl.BlockSpec(memory_space=pltpu.VMEM)] * 2,
        scratch_shapes=[
            scratch(3, 16, 16, 128),
            pltpu.VMEM((9, 32), BF16),
            scratch(1, 32),
            pltpu.VMEM((32, 32), BF16),
            scratch(1, 32),
            pltpu.VMEM((1, 32), BF16),
            pltpu.VMEM((256, 80), BF16),
            pltpu.VMEM((256, 256), BF16),
            pltpu.VMEM((16, 256), BF16),
            scratch(256, 128),
            scratch(256, 128),
            scratch(3, plane_buffer, 128),
            scratch(plane_buffer, 128),
            scratch(3, plane_buffer, 128),
            scratch(4, 3, 16, 128),
            scratch(3, 16, 128),
            scratch(2, 2, 8, 128),
            scratch(4, 3, 16, 128),
            scratch(2, 4, 32, 128),
            scratch(2, 2, 8, 128),
            scratch(2, 2, 4, 16, 128),
            scratch(4, 16, 128),
            scratch(16, 128),
            scratch(2, 2, 8, 128),
            scratch(4, 16, 128),
            scratch(2, 2, 8, 128),
            scratch(4, 32, 128),
            scratch(4, plane_buffer, 128),
            scratch(16, 16, 128),
            scratch(256, 128),
            scratch(2, 6, 16, 128),
            scratch(2, 2, 16, 128),
            scratch(2, 16, 128),
            scratch(2, 6, 16, 128),
            scratch(2, 6, 16, 128),
            scratch(2, 2, 16, 128),
            scratch(2, 4, 32, 128),
            scratch(2, level0, 128),
            scratch(2, level0, 128),
            scratch(2, level0, 128),
            scratch(384, 256),
            scratch(384, 128),
            scratch(192, 128),
            scratch(192, 128),
            scratch(8, 8, 128),
            scratch(8, 128),
            scratch(2, 5, 8, 128),
            scratch(2, 8, 8, 128),
            scratch(2, 2, 5, 8, 128),
            scratch(2, 3, 24, 128),
            scratch(432, 128),
            scratch(432, 128),
            scratch(432, 128),
            scratch(4, 128),
            scratch(7, 3, 4, 128),
            scratch(2, 32, 128),
            scratch(7, 2, 32, 128),
            scratch(896, 128),
            scratch(896, 128),
            scratch(896, 128),
            scratch(192, 128),
            scratch(192, 128),
            scratch(192, 128),
            pltpu.SemaphoreType.DMA((N_COPIES,)),
            pltpu.SemaphoreType.DMA((N_COPIES,)),
            pltpu.SemaphoreType.DMA((6,)),
        ],
        compiler_params=pltpu.CompilerParams(
            collective_id=0, has_side_effects=True, vmem_limit_bytes=60 * 1024 * 1024
        ),
    )(
        velocity,
        input_weight.T,
        input_bias.reshape(1, 32),
        hidden_weight,
        hidden_bias.reshape(1, 32),
        output_weight.reshape(1, 32),
    )
    return pl.pallas_call(
        hand_over,
        out_shape=(
            jax.ShapeDtypeStruct((3, 16, 16, 128), F32),
            jax.ShapeDtypeStruct((16, 16, 128), F32),
        ),
        in_specs=[pl.BlockSpec(memory_space=pl.ANY)] * 2,
        out_specs=[pl.BlockSpec(memory_space=pl.ANY)] * 2,
        scratch_shapes=[pltpu.SemaphoreType.DMA((2,))],
        compiler_params=pltpu.CompilerParams(vmem_limit_bytes=1024 * 1024),
    )(*results)


def solution(mesh):
    return jax.shard_map(
        body,
        mesh=mesh,
        in_specs=(P(None, "gx", "gy", "gz"), P(), P(), P(), P(), P()),
        out_specs=(P(None, "gx", "gy", "gz"), P("gx", "gy", "gz")),
        check_vma=False,
    )
```

```python
import jax
import jax.numpy as jnp
from jax import lax
from jax.experimental import pallas as pl
from jax.experimental.pallas import tpu as pltpu
from jax.sharding import PartitionSpec as P

MESH = pl.DeviceIdType.MESH
AXES = ("gx", "gy", "gz")
F32, BF16 = jnp.float32, jnp.bfloat16

TIME_STEP = 0.1
GAIN = 0.5
C = 0.8 / 6.0

FACES = [(1, 0, 0), (-1, 0, 0), (0, 1, 0), (0, -1, 0), (0, 0, 1), (0, 0, -1)]
AROUND = [
    (i, j, k) for i in (-1, 0, 1) for j in (-1, 0, 1) for k in (-1, 0, 1) if (i, j, k) != (0, 0, 0)
]
PLANE_ROWS = 24
NEAR = [(a, b) for a in range(5) for b in range(5) if a + b <= 4]
CORNER = [(i, j, k, o) for i in (0, 1) for j in (0, 1) for k, o in enumerate(NEAR)]
EDGES = [o for o in AROUND if abs(o[0]) + abs(o[1]) + abs(o[2]) == 2]
N_COPIES = 6 + 16 + 20 + 26 * 2 + 20 + 6


def at(x, y=0):
    return 8 + PLANE_ROWS * (x + 2) + y


def column(y):
    return pl.ds(at(0, y), 16, stride=PLANE_ROWS)


def at0(p):
    return 8 + 32 * p


def lanes(shape):
    return lax.broadcasted_iota(jnp.int32, shape, len(shape) - 1)


def rows_of(shape):
    return lax.broadcasted_iota(jnp.int32, shape, len(shape) - 2)


def lane_roll(value, shift):
    return pltpu.roll(value, shift % 128, value.ndim - 1)


def dot(a, b, precision=None):
    return jnp.dot(a, b, precision=precision, preferred_element_type=F32)


def coarse_lane(shape, axis):
    fine = lax.broadcasted_iota(jnp.int32, shape, axis)
    return jnp.where(fine < 192, 32 + fine // 2, fine // 2 - 96)


def exact_dot(a, b):
    b = b.astype(BF16)
    first = a.astype(BF16)
    rest = a - first.astype(F32)
    second = rest.astype(BF16)
    third = (rest - second.astype(F32)).astype(BF16)
    return dot(third, b) + dot(second, b) + dot(first, b)


class Copies:
    def __init__(self, ids, send_sem, recv_sem):
        self.ids, self.send_sem, self.recv_sem = ids, send_sem, recv_sem
        self.made, self.count = [], 0

    def device(self, offset):
        return tuple(lax.rem(i + 8 + o, 8) for i, o in zip(self.ids, offset))

    def start(self, src, dst, offset):
        k = self.count + len(self.made)
        copy = pltpu.make_async_remote_copy(
            src_ref=src,
            dst_ref=dst,
            send_sem=self.send_sem.at[k],
            recv_sem=self.recv_sem.at[k],
            device_id=self.device(offset),
            device_id_type=MESH,
        )
        copy.start()
        self.made.append(copy)
        return copy

    def sent(self):
        for copy in self.made:
            copy.wait_send()
        self.count += len(self.made)
        self.made = []


def sum6(ref, base, n, period):
    center = ref[pl.ds(base, n), :]
    total = ref[pl.ds(base + period, n), :] + ref[pl.ds(base - period, n), :]
    total = total + ref[pl.ds(base + 1, n), :] + ref[pl.ds(base - 1, n), :]
    return center, total + lane_roll(center, 1) + lane_roll(center, -1)


def sum6_wide(ref, base, n, period):
    center = [ref[t, pl.ds(base, n), :] for t in (0, 1)]
    lane = lanes((n, 128))
    up = [lane_roll(c, -1) for c in center]
    down = [lane_roll(c, 1) for c in center]
    out = []
    for t in (0, 1):
        total = ref[t, pl.ds(base + period, n), :] + ref[t, pl.ds(base - period, n), :]
        total = total + ref[t, pl.ds(base + 1, n), :] + ref[t, pl.ds(base - 1, n), :]
        total = total + jnp.where(lane == 127, up[1 - t], up[t])
        out.append(total + jnp.where(lane == 0, down[1 - t], down[t]))
    return center, out


def kernel(
    vel_in, w1_in, b1_in, w2_in, b2_in, w3_in, vout, pout,
    vel, w1, b1, w2, b2, w3, w1k, w2k, w3k, b1k, b2k,
    vb, nb, pb, sy, sz, sxy, ry, rz, rxy, rxz, syn, szn, sxyn, ryn, rxyn, cz, zb,
    dv, dvr, sdy, sde, sdz, rdx, rdy, rde, rdz, db, v0, u0,
    rs, rt, s1, v1s, r1c, sez, rex, rey, ree, rez, lb1, v1, u1,
    sa, ra, sb, rb, lb2, v2, u2, lb3, v3, u3,
    send_sem, recv_sem, load_sem,
):
    ids = [lax.axis_index(a) for a in AXES]
    cp = Copies(ids, send_sem, recv_sem)
    barrier = pltpu.get_barrier_semaphore()
    for offset in FACES:
        pl.semaphore_signal(barrier, inc=1, device_id=cp.device(offset), device_id_type=MESH)

    loads = [
        pltpu.make_async_copy(src, dst, load_sem.at[k])
        for k, (src, dst) in enumerate(
            ((vel_in, vel), (w1_in, w1), (b1_in, b1), (w2_in, w2), (b2_in, b2), (w3_in, w3))
        )
    ]
    for load in loads:
        load.start()
    loads[0].wait()
    for c in range(3):
        for x in range(16):
            vb[c, pl.ds(at(x), 16), :] = vel[c, x]

    lane16 = lanes((16, 128))

    def pack_z(plane_of):
        packed = jnp.zeros((16, 128), F32)
        for x in range(16):
            plane = plane_of(x)
            packed = jnp.where(lane16 // 2 == 4 * x + 1, lane_roll(plane, 8 * x + 2), packed)
            packed = jnp.where(lane16 // 2 == 4 * x + 2, lane_roll(plane, 8 * x + 6), packed)
        return packed

    for c in range(3):
        for k, y in enumerate((0, 1, 14, 15)):
            sy[k, c] = vb[c, column(y), :]
        sz[c] = pack_z(lambda x: vel[c, x])
        for i in (0, 1):
            for j in (0, 1):
                sxy[i, j, pl.ds(c, 1), :] = vel[c, 15 * i, pl.ds(15 * j, 1), :]

    pl.semaphore_wait(barrier, len(FACES))

    vel_copies = [
        cp.start(sz, rz.at[0, pl.ds(0, 3), pl.ds(8, 16), :], (0, 0, 1)),
        cp.start(sz, rz.at[1, pl.ds(0, 3), pl.ds(8, 16), :], (0, 0, -1)),
        cp.start(sy.at[3], ry.at[1], (0, 1, 0)),
        cp.start(sy.at[0], ry.at[2], (0, -1, 0)),
        cp.start(vel.at[:, 15], vb.at[:, pl.ds(at(-1), 16), :], (1, 0, 0)),
        cp.start(vel.at[:, 0], vb.at[:, pl.ds(at(16), 16), :], (-1, 0, 0)),
    ]

    for load in loads[1:]:
        load.wait()
    spread = (rows_of((256, 32)) // 8 == lanes((256, 32))).astype(BF16)
    spread_t = (rows_of((32, 256)) == lanes((32, 256)) // 8).astype(BF16)
    columns = (rows_of((80, 9)) // 8 == lanes((80, 9))).astype(BF16)
    wide = lax.dot_general(
        spread, dot(columns, w1[...]).astype(BF16), (((1,), (1,)), ((), ())), preferred_element_type=F32
    )
    same = rows_of((256, 80)) % 8 == lanes((256, 80)) % 8
    w1k[...] = jnp.where(same, wide, 0.0).astype(BF16)
    wide = dot(dot(spread, w2[...]).astype(BF16), spread_t)
    same = rows_of((256, 256)) % 8 == lanes((256, 256)) % 8
    w2k[...] = jnp.where(same, wide, 0.0).astype(BF16)
    wide = jnp.broadcast_to(dot(w3[...], spread_t), (16, 256))
    same = rows_of((16, 256)) == lanes((16, 256)) % 8
    w3k[...] = jnp.where(same, wide, 0.0).astype(BF16)
    mine = rows_of((256, 32)) // 8 == lanes((256, 32))
    for bias, kept in ((b1, b1k), (b2, b2k)):
        bias_column = jnp.sum(jnp.where(mine, bias[...], 0.0), axis=1, keepdims=True)
        kept[...] = jnp.broadcast_to(bias_column, (256, 128))
    lb2[...] = jnp.zeros_like(lb2)
    for p in range(28):
        for first in (0, 24):
            db[0, pl.ds(at0(p) + first, 8), :] = jnp.zeros((8, 128), F32)
    for c in vel_copies:
        c.wait_recv()
    for c in range(3):
        vb[c, column(-1), :] = ry[1, c]
        vb[c, column(16), :] = ry[2, c]

    for first_x in range(0, 16, 8):
        listing = [[] for _ in range(10)]
        for x in range(first_x, first_x + 8):
            base = at(x)
            g = []
            for c in range(3):
                plane = vb[c, pl.ds(base, 16), :]
                after = lane_roll(rz[1, c, pl.ds(8, 16), :], 125 - 8 * x)
                before = lane_roll(rz[0, c, pl.ds(8, 16), :], -(8 * x + 5))
                after = jnp.where(lane16 == 127, after, lane_roll(plane, -1))
                before = jnp.where(lane16 == 0, before, lane_roll(plane, 1))
                around = [
                    (vb[c, pl.ds(base + step, 16), :], vb[c, pl.ds(base - step, 16), :])
                    for step in (PLANE_ROWS, 1)
                ]
                g.append([0.5 * (a - b) for a, b in around + [(after, before)]])
            entries = [
                g[0][0], g[1][1], g[2][2],
                0.5 * (g[0][1] + g[1][0]), 0.5 * (g[0][2] + g[2][0]), 0.5 * (g[1][2] + g[2][1]),
                0.5 * (g[0][1] - g[1][0]), 0.5 * (g[0][2] - g[2][0]), 0.5 * (g[1][2] - g[2][1]),
                jnp.zeros((16, 128), F32),
            ]
            for tiles, entry in zip(listing, entries):
                tiles += [entry[0:8], entry[8:16]]
        features = jnp.concatenate(
            [jnp.concatenate(tiles, axis=1) for tiles in listing], axis=0
        ).astype(BF16)
        if first_x == 0:
            more_copies = []
            for dx, dy, dz in EDGES:
                i, j, k = (1 - dx) // 2, (1 - dy) // 2, (1 - dz) // 2
                if dz == 0:
                    src, dst = sxy.at[1 - i, 1 - j], rxy.at[i, j]
                elif dy == 0:
                    src, dst = sz, rxz.at[k, i, pl.ds(0, 3)]
                else:
                    part, rows = pl.ds(8 * (1 - j), 8), pl.ds(24 * j, 8)
                    src, dst = sz.at[:, part, :], rz.at[k, pl.ds(0, 3), rows, :]
                more_copies.append(cp.start(src, dst, (dx, dy, dz)))
            more_copies += [
                cp.start(sy.at[2], ry.at[0], (0, 1, 0)),
                cp.start(sy.at[1], ry.at[3], (0, -1, 0)),
                cp.start(vel.at[:, 14], vb.at[:, pl.ds(at(-2), 16), :], (1, 0, 0)),
                cp.start(vel.at[:, 1], vb.at[:, pl.ds(at(17), 16), :], (-1, 0, 0)),
            ]
        bias = jnp.concatenate([b1k[...]] * 16, axis=1)
        hidden = jnp.tanh(dot(w1k[...], features) + bias).astype(BF16)
        bias = jnp.concatenate([b2k[...]] * 16, axis=1)
        second = jnp.tanh(dot(w2k[...], hidden) + bias).astype(BF16)
        s = dot(w3k[...], second)[0:8]
        soft = GAIN * (jnp.maximum(s, 0.0) + jnp.log1p(jnp.exp(-jnp.abs(s))))
        for k in range(16):
            nb[pl.ds(at(first_x + k // 2, 8 * (k % 2)), 8), :] = soft[:, 128 * k : 128 * k + 128]

    for k, y in enumerate((0, 1, 14, 15)):
        syn[k] = nb[column(y), :]
    szn[...] = pack_z(lambda x: nb[pl.ds(at(x), 16), :])
    for i in (0, 1):
        for j in (0, 1):
            sxyn[i, j, pl.ds(0, 1), :] = nb[pl.ds(at(15 * i, 15 * j), 1), :]
    visc_copies = []
    for dx, dy, dz in EDGES:
        i, j, k = (1 - dx) // 2, (1 - dy) // 2, (1 - dz) // 2
        if dz == 0:
            src, dst = sxyn.at[1 - i, 1 - j], rxyn.at[i, j]
        elif dy == 0:
            src, dst = szn, rxz.at[k, i, 3]
        else:
            part, rows = pl.ds(8 * (1 - j), 8), pl.ds(24 * j, 8)
            src, dst = szn.at[part, :], rz.at[k, 3, rows, :]
        visc_copies.append(cp.start(src, dst, (dx, dy, dz)))
    visc_copies += [
        cp.start(szn, rz.at[0, 3, pl.ds(8, 16), :], (0, 0, 1)),
        cp.start(szn, rz.at[1, 3, pl.ds(8, 16), :], (0, 0, -1)),
        cp.start(syn.at[pl.ds(2, 2)], ryn.at[pl.ds(0, 2)], (0, 1, 0)),
        cp.start(syn.at[pl.ds(0, 2)], ryn.at[pl.ds(2, 2)], (0, -1, 0)),
    ]
    for x in (14, 15):
        here, there = pl.ds(at(x), 16), pl.ds(at(x - 16), 16)
        visc_copies.append(cp.start(nb.at[here, :], nb.at[there, :], (1, 0, 0)))
    for x in (0, 1):
        here, there = pl.ds(at(x), 16), pl.ds(at(x + 16), 16)
        visc_copies.append(cp.start(nb.at[here, :], nb.at[there, :], (-1, 0, 0)))

    slot = lanes((32, 128)) % 8

    def beyond(f, own):
        none = jnp.zeros((8, 128), F32)
        whole = jnp.concatenate([none, own, none], axis=0)
        outer = jnp.where(slot < 4, lane_roll(rz[0, f], -4), lane_roll(rz[1, f], 4))
        whole = jnp.where((slot >= 2) & (slot < 6), whole, outer)
        cz[f] = whole
        ends = jnp.where(slot == 0, lane_roll(whole, -1), lane_roll(whole, -5))
        for x in range(16):
            zb[f, pl.ds(at(x, -4), 24), :] = lane_roll(ends, -(8 * x + 1))[4:28]
        zb[f, pl.ds(at(-1), 16), :] = jnp.where(
            lane16 == 127, lane_roll(rxz[0, 0, f], 2), lane_roll(rxz[1, 0, f], 6)
        )
        zb[f, pl.ds(at(16), 16), :] = jnp.where(
            lane16 == 127, lane_roll(rxz[0, 1, f], 122), lane_roll(rxz[1, 1, f], -2)
        )

    for c in more_copies:
        c.wait_recv()
    for c in range(3):
        vb[c, column(-2), :] = ry[0, c]
        vb[c, column(17), :] = ry[3, c]
        for i in (0, 1):
            for j in (0, 1):
                vb[c, pl.ds(at(17 * i - 1, 17 * j - 1), 1), :] = rxy[i, j, pl.ds(c, 1), :]
        beyond(c, sz[c])
    for c in visc_copies:
        c.wait_recv()
    for k, y in enumerate((-2, -1, 16, 17)):
        nb[column(y), :] = ryn[k]
    for i in (0, 1):
        for j in (0, 1):
            nb[pl.ds(at(17 * i - 1, 17 * j - 1), 1), :] = rxyn[i, j, pl.ds(0, 1), :]
    beyond(3, szn[...])

    def change(i, n_mid, n_near, v_mid, v_near):
        total = 0.0
        for j in range(3):
            (up, down), (up_j, down_j) = v_near[i][j], v_near[j][j]
            total = total + 0.5 * (n_mid + n_near[j][0]) * (up - v_mid[i])
            total = total - 0.5 * (n_mid + n_near[j][1]) * (v_mid[i] - down)
            total = total - 0.5 * (up_j * up - down_j * down)
        return v_mid[i] + TIME_STEP * total

    def near(load, ends, start, n):
        mid = load(start)
        lane = lanes((n, 128))
        return mid, [
            (load(start + PLANE_ROWS), load(start - PLANE_ROWS)),
            (load(start + 1), load(start - 1)),
            (
                lane_roll(jnp.where(lane == 0, ends, mid), -1),
                lane_roll(jnp.where(lane == 127, ends, mid), 1),
            ),
        ]

    def tendency(start, n, components):
        where = pl.ds(start, n)
        n_mid, n_near = near(lambda r: nb[pl.ds(r, n), :], zb[3, where, :], start, n)
        both = [near(lambda r, c=c: vb[c, pl.ds(r, n), :], zb[c, where, :], start, n) for c in range(3)]
        for i in components:
            pb[i, where, :] = change(i, n_mid, n_near, [b[0] for b in both], [b[1] for b in both])

    for x in range(16):
        tendency(at(x), 16, (0, 1, 2))
    tendency(at(-1), 16, (0,))
    tendency(at(16), 16, (0,))
    for x in range(-1, 16):
        tendency(at(x, 16), 8, (1,))

    def near_end(f):
        mid = cz[f, pl.ds(8, 16), :]
        above = jnp.where(lane16 == 126, lane_roll(rxz[1, 1, f], 124), lane_roll(rxz[0, 1, f], 116))
        below = jnp.where(lane16 == 6, lane_roll(rxz[1, 0, f], 12), lane_roll(rxz[0, 0, f], 4))
        return mid, [
            (
                jnp.where(lane16 >= 120, above, lane_roll(mid, -8)),
                jnp.where(lane16 < 8, below, lane_roll(mid, 8)),
            ),
            (cz[f, pl.ds(9, 16), :], cz[f, pl.ds(7, 16), :]),
            (lane_roll(mid, -1), lane_roll(mid, 1)),
        ]

    fields = [near_end(f) for f in range(4)]
    far = change(2, *fields[3], [f[0] for f in fields[:3]], [f[1] for f in fields[:3]])
    far = jnp.where(lane16 % 8 == 0, lane_roll(far, -1), lane_roll(far, -5))

    for x in range(16):
        base = at(x)
        plane, ends = pb[2, pl.ds(base, 16), :], lane_roll(far, -(8 * x + 1))
        total = pb[0, pl.ds(base + PLANE_ROWS, 16), :] - pb[0, pl.ds(base - PLANE_ROWS, 16), :]
        total = total + pb[1, pl.ds(base + 1, 16), :] - pb[1, pl.ds(base - 1, 16), :]
        total = total + lane_roll(jnp.where(lane16 == 0, ends, plane), -1)
        dv[x] = 0.5 * (total - lane_roll(jnp.where(lane16 == 127, ends, plane), 1))
        dvr[pl.ds(16 * x, 16), :] = dv[x]

    for half in range(2):
        packed = jnp.zeros((16, 128), F32)
        for k in range(8):
            packed = jnp.where(lane16 // 16 == k, lane_roll(dv[8 * half + k], 16 * k + 8), packed)
        sdz[half] = packed
    for y in range(6):
        for j, first in enumerate((0, 10)):
            sdy[j, y] = dvr[pl.ds(first + y, 16, stride=16), :]
    for i, j, k, (a, b) in CORNER:
        x, y = (15 - a if i else a), (15 - b if j else b)
        sde[i, j, pl.ds(k, 1), :] = dvr[pl.ds(16 * x + y, 1), :]
    div_copies = []
    for dx, dy, dz in AROUND:
        here_x, here_y = (1 - dx) // 2, (1 - dy) // 2
        if dz == 0:
            if dy == 0:
                src, dst = dv.at[pl.ds(10 if dx > 0 else 0, 6)], rdx.at[here_x]
            elif dx == 0:
                src, dst = sdy.at[1 - here_y], rdy.at[here_y]
            else:
                src, dst = sde.at[1 - here_x, 1 - here_y], rde.at[here_x, here_y]
        else:
            half = pl.ds(0, 2) if dx == 0 else pl.ds(1 if dx > 0 else 0, 1)
            slot = pl.ds(1, 2) if dx == 0 else pl.ds(0 if dx > 0 else 3, 1)
            part = pl.ds(0, 16) if dy == 0 else pl.ds(8 if dy > 0 else 0, 8)
            rows = pl.ds(8, 16) if dy == 0 else pl.ds(0 if dy > 0 else 24, 8)
            src, dst = sdz.at[half, part, :], rdz.at[(1 - dz) // 2, slot, rows, :]
        div_copies.append(cp.start(src, dst, (dx, dy, dz)))

    for x in range(16):
        db[0, pl.ds(at0(x + 6) + 8, 16), :] = dv[x]
    for c in div_copies:
        c.wait_recv()
    for x in range(6):
        for side, p in ((0, x), (1, 22 + x)):
            db[0, pl.ds(at0(p) + 8, 16), :] = rdx[side, x]
    for i, j, k, (a, b) in CORNER:
        p, y = (22 + a if i else 5 - a), (16 + b if j else -1 - b)
        db[0, pl.ds(at0(p) + 8 + y, 1), :] = rde[i, j, pl.ds(k, 1), :]
    for y in range(6):
        db[0, pl.ds(at0(6) + 2 + y, 16, stride=32), :] = rdy[0, y]
        db[0, pl.ds(at0(6) + 24 + y, 16, stride=32), :] = rdy[1, y]
    lane32 = lanes((32, 128))
    for g in range(4):
        both = jnp.where(lane32 % 16 < 8, rdz[0, g], rdz[1, g])
        for k in range(8):
            x = 8 * (g - 1) + k
            if -6 <= x < 22:
                db[1, pl.ds(at0(x + 6), 32), :] = lane_roll(both, -(16 * k + 8))

    for p in range(1, 27, 2):
        b, around = sum6_wide(db, at0(p), 64, 32)
        for t in (0, 1):
            v0[t, pl.ds(at0(p), 64), :] = -C * (1.2 * b[t] + C * around[t])
    for k in range(12):
        for edge in (0, 24):
            rs[pl.ds(32 * k + edge, 8), :] = jnp.zeros((8, 256), F32)
        pair = [0.0, 0.0]
        for base in (at0(2 + 2 * k) + 4, at0(3 + 2 * k) + 4):
            v, around = sum6_wide(v0, base, 24, 32)
            for t in (0, 1):
                pair[t] = pair[t] + db[t, pl.ds(base, 24), :] - (around[t] - 6.0 * v[t])
        for t in (0, 1):
            rs[pl.ds(32 * k + 4, 24), pl.ds(128 * t, 128)] = pair[t]
    halve = jnp.where(coarse_lane((256, 128), 0) == lanes((256, 128)), 0.125, 0.0).astype(F32)
    rt[...] = exact_dot(rs[...], halve)
    s1[...] = rt[pl.ds(0, 192, stride=2), :] + rt[pl.ds(1, 192, stride=2), :]

    lane8 = lanes((8, 128))
    packed = jnp.zeros((8, 128), F32)
    for x in range(8):
        plane = s1[pl.ds(16 * (x + 2) + 4, 8), :]
        r1c[x] = plane
        packed = jnp.where(lane8 // 8 == 2 * x, lane_roll(plane, 16 * x - 88), packed)
        packed = jnp.where(lane8 // 8 == 2 * x + 1, lane_roll(plane, 16 * x + 8 - 32), packed)
    sez[...] = packed

    for p in range(1, 11, 5):
        b, around = sum6(s1, 16 * p, 80, 16)
        v1s[pl.ds(16 * p, 80), :] = -4.0 * C * (1.2 * b + C * around)
    parts = []
    for k in range(4):
        base = 16 * (2 + 2 * k)
        v, around = sum6(v1s, base, 32, 16)
        residual = s1[pl.ds(base, 32), :] - 0.25 * (around - 6.0 * v)
        parts.append(residual[0:16] + residual[16:32])
    halve = halve[0:128]
    rt[pl.ds(0, 64), :] = exact_dot(jnp.concatenate(parts, axis=0), halve)
    packed = jnp.zeros((8, 128), F32)
    for x in range(4):
        plane = rt[pl.ds(16 * x, 8, stride=2), :] + rt[pl.ds(16 * x + 1, 8, stride=2), :]
        packed = jnp.where(lane8 // 32 == x, lane_roll(plane, 32 * x - 48), packed)
    sa[...] = packed[2:6]
    ra[3, 1] = packed[2:6]
    yz_copies = [
        cp.start(sa, ra.at[3 - dy, 1 - dz], (0, dy, dz))
        for dy in (3, -3, 2, -2, 1, -1, 0)
        for dz in (1, -1, 0)
        if (dy, dz) != (0, 0)
    ]
    src_copies = []
    for dx, dy, dz in AROUND:
        here_x, here_y = (1 - dx) // 2, (1 - dy) // 2
        if dz == 0:
            planes = pl.ds(3 if dx > 0 else 0, 5)
            if dy == 0:
                src, dst = r1c.at[planes], rex.at[here_x]
            elif dx == 0:
                src, dst = r1c, rey.at[here_y]
            else:
                src, dst = r1c.at[planes], ree.at[here_x, here_y]
        else:
            src, dst = sez, rez.at[(1 - dz) // 2, 1 - dx, pl.ds(8 * (1 - dy), 8), :]
        src_copies.append(cp.start(src, dst, (dx, dy, dz)))

    for c in yz_copies:
        c.wait_recv()
    lane4 = lanes((4, 128))
    for dy in range(7):
        for x in range(4):
            before, here, after = (
                lane_roll(ra[dy, k], lane - 32 * x) for k, lane in ((0, 16), (1, 48), (2, 80))
            )
            whole = jnp.where(lane4 < 48, before, jnp.where(lane4 < 80, here, after))
            lb2[pl.ds(32 * (12 + x) + 4 * dy, 4), :] = whole
    lane32 = lanes((32, 128))
    for k in range(2):
        left, right = lb2[pl.ds(32 * (12 + 2 * k), 32), :], lb2[pl.ds(32 * (13 + 2 * k), 32), :]
        sb[k] = jnp.where(lane32 < 64, lane_roll(left, -32), lane_roll(right, 32))
    x_copies = []
    for dx in (3, -3, 2, -2, 1, -1):
        rows = pl.ds(0, 24 if abs(dx) == 3 else 32)
        x_copies.append(cp.start(sb.at[:, rows, :], rb.at[3 - dx, :, rows, :], (dx, 0, 0)))

    for c in src_copies:
        c.wait_recv()
    lane24 = lanes((24, 128))
    for p in range(18):
        dx, x = (p - 5) // 8, (p - 5) % 8
        if dx == 0:
            three = [rey[0, x], r1c[x], rey[1, x]]
        else:
            side = (dx + 1) // 2
            k = x - 3 if dx < 0 else x
            three = [ree[side, 0, k], rex[side, k], ree[side, 1, k]]
        before = lane_roll(rez[0, dx + 1], 24 - 16 * x)
        after = lane_roll(rez[1, dx + 1], 96 - 16 * x - 8)
        here = jnp.concatenate(three, axis=0)
        lb1[pl.ds(24 * p, 24), :] = jnp.where(
            lane24 < 32, before, jnp.where(lane24 < 96, here, after)
        )
    for p in range(1, 17, 4):
        b, around = sum6(lb1, 24 * p, 96, 24)
        v1[pl.ds(24 * p, 96), :] = -4.0 * C * (1.2 * b + C * around)

    cp.sent()
    for c in x_copies:
        c.wait_recv()
    for dx in (-3, -2, -1, 1, 2, 3):
        n = 24 if abs(dx) == 3 else 32
        for x in range(4):
            plane = lane_roll(rb[3 + dx, x // 2, pl.ds(0, n), :], 32 if x % 2 == 0 else -32)
            lb2[pl.ds(32 * (4 * (3 + dx) + x), n), :] = plane

    for p in range(1, 27, 2):
        b, around = sum6(lb2, 32 * p, 64, 32)
        v2[pl.ds(32 * p, 64), :] = -16.0 * C * (1.2 * b + C * around)
    for k in range(12):
        base = 32 * (2 + 2 * k)
        v, around = sum6(v2, base, 64, 32)
        residual = lb2[pl.ds(base, 64), :] - 0.0625 * (around - 6.0 * v)
        rs[pl.ds(32 * k, 32), pl.ds(0, 128)] = residual[0:32] + residual[32:64]
    rt[...] = exact_dot(rs[:, 0:128], halve)
    lb3[...] = rt[pl.ds(0, 192, stride=2), :] + rt[pl.ds(1, 192, stride=2), :]

    b, around = sum6(lb3, 16, 160, 16)
    v3[pl.ds(16, 160), :] = -64.0 * C * (1.2 * b + C * around)
    v, around = sum6(v3, 32, 128, 16)
    u3[pl.ds(32, 128), :] = 0.2 * v + C * around - 64.0 * C * lb3[pl.ds(32, 128), :]
    v, around = sum6(u3, 48, 96, 16)
    coarse = 0.2 * v + C * around - 64.0 * C * lb3[pl.ds(48, 96), :]

    double = jnp.where(rows_of((128, 256)) == coarse_lane((128, 256), 1), 1.0, 0.0).astype(F32)
    fine = exact_dot(coarse, double[:, 0:128])
    for k in range(6):
        for p in (8 + 2 * k, 9 + 2 * k):
            for odd in (0, 1):
                where = pl.ds(32 * p + odd, 16, stride=2)
                v2[where, :] = v2[where, :] + fine[16 * k : 16 * k + 16]
    for p in range(9, 19):
        where = pl.ds(32 * p + 8, 16)
        v, around = sum6(v2, 32 * p + 8, 16, 32)
        u2[where, :] = 0.2 * v + C * around - 16.0 * C * lb2[where, :]
    for k in range(8):
        base = 32 * (10 + k) + 8
        v, around = sum6(u2, base, 16, 32)
        rs[pl.ds(16 * k, 16), pl.ds(0, 128)] = (
            0.2 * v + C * around - 16.0 * C * lb2[pl.ds(base, 16), :]
        )

    fine = exact_dot(rs[0:128, 0:128], double[:, 0:128])
    for k in range(8):
        for p in (1 + 2 * k, 2 + 2 * k):
            for odd in (0, 1):
                where = pl.ds(24 * p + odd, 12, stride=2)
                v1[where, :] = v1[where, :] + fine[16 * k : 16 * k + 12]
    for p in range(2, 16, 2):
        v, around = sum6(v1, 24 * p, 48, 24)
        u1[pl.ds(24 * p, 48), :] = 0.2 * v + C * around - 4.0 * C * lb1[pl.ds(24 * p, 48), :]
    for k in range(12):
        base = 24 * (3 + k) + 4
        v, around = sum6(u1, base, 16, 24)
        rs[pl.ds(16 * k, 16), pl.ds(0, 128)] = (
            0.2 * v + C * around - 4.0 * C * lb1[pl.ds(base, 16), :]
        )

    for t in (0, 1):
        fine = exact_dot(rs[0:192, 0:128], double[:, 128 * t : 128 * t + 128])
        for k in range(12):
            for p in (2 + 2 * k, 3 + 2 * k):
                for odd in (0, 1):
                    where = pl.ds(at0(p) + odd, 16, stride=2)
                    v0[t, where, :] = v0[t, where, :] + fine[16 * k : 16 * k + 16]
    for p in range(4, 24):
        base = at0(p) + 4
        v, around = sum6_wide(v0, base, 24, 32)
        for t in (0, 1):
            b = db[t, pl.ds(base, 24), :]
            u0[t, pl.ds(base, 24), :] = 0.2 * v[t] + C * around[t] - C * b
    for p in range(5, 23):
        base = at0(p) + 4
        v, around = sum6_wide(u0, base, 24, 32)
        for t in (0, 1):
            b = db[t, pl.ds(base, 24), :]
            v0[t, pl.ds(base, 24), :] = 0.2 * v[t] + C * around[t] - C * b

    for x in range(16):
        base = at0(x + 6) + 8
        here, beyond = v0[0, pl.ds(base, 16), :], v0[1, pl.ds(base, 16), :]
        pout[x] = here
        slopes = [
            v0[0, pl.ds(base + 32, 16), :] - v0[0, pl.ds(base - 32, 16), :],
            v0[0, pl.ds(base + 1, 16), :] - v0[0, pl.ds(base - 1, 16), :],
            jnp.where(lane16 == 127, lane_roll(beyond, -1), lane_roll(here, -1))
            - jnp.where(lane16 == 0, lane_roll(beyond, 1), lane_roll(here, 1)),
        ]
        for c in range(3):
            vout[c, x] = pb[c, pl.ds(at(x), 16), :] - 0.5 * slopes[c]


def hand_over(velocity, pressure, velocity_out, pressure_out, sem):
    first = pltpu.make_async_copy(velocity, velocity_out, sem.at[0])
    second = pltpu.make_async_copy(pressure, pressure_out, sem.at[1])
    first.start()
    second.start()
    first.wait()
    second.wait()


def body(velocity, input_weight, input_bias, hidden_weight, hidden_bias, output_weight):
    def scratch(*shape):
        return pltpu.VMEM(shape, F32)

    plane_buffer = 16 + PLANE_ROWS * 20
    level0 = 16 + 32 * 28
    results = pl.pallas_call(
        kernel,
        out_shape=(
            pltpu.VMEM((3, 16, 16, 128), F32),
            pltpu.VMEM((16, 16, 128), F32),
        ),
        in_specs=[pl.BlockSpec(memory_space=pltpu.HBM)] * 6,
        out_specs=[pl.BlockSpec(memory_space=pltpu.VMEM)] * 2,
        scratch_shapes=[
            scratch(3, 16, 16, 128),
            pltpu.VMEM((9, 32), BF16),
            scratch(1, 32),
            pltpu.VMEM((32, 32), BF16),
            scratch(1, 32),
            pltpu.VMEM((1, 32), BF16),
            pltpu.VMEM((256, 80), BF16),
            pltpu.VMEM((256, 256), BF16),
            pltpu.VMEM((16, 256), BF16),
            scratch(256, 128),
            scratch(256, 128),
            scratch(3, plane_buffer, 128),
            scratch(plane_buffer, 128),
            scratch(3, plane_buffer, 128),
            scratch(4, 3, 16, 128),
            scratch(3, 16, 128),
            scratch(2, 2, 8, 128),
            scratch(4, 3, 16, 128),
            scratch(2, 4, 32, 128),
            scratch(2, 2, 8, 128),
            scratch(2, 2, 4, 16, 128),
            scratch(4, 16, 128),
            scratch(16, 128),
            scratch(2, 2, 8, 128),
            scratch(4, 16, 128),
            scratch(2, 2, 8, 128),
            scratch(4, 32, 128),
            scratch(4, plane_buffer, 128),
            scratch(16, 16, 128),
            scratch(256, 128),
            scratch(2, 6, 16, 128),
            scratch(2, 2, 16, 128),
            scratch(2, 16, 128),
            scratch(2, 6, 16, 128),
            scratch(2, 6, 16, 128),
            scratch(2, 2, 16, 128),
            scratch(2, 4, 32, 128),
            scratch(2, level0, 128),
            scratch(2, level0, 128),
            scratch(2, level0, 128),
            scratch(384, 256),
            scratch(384, 128),
            scratch(192, 128),
            scratch(192, 128),
            scratch(8, 8, 128),
            scratch(8, 128),
            scratch(2, 5, 8, 128),
            scratch(2, 8, 8, 128),
            scratch(2, 2, 5, 8, 128),
            scratch(2, 3, 24, 128),
            scratch(432, 128),
            scratch(432, 128),
            scratch(432, 128),
            scratch(4, 128),
            scratch(7, 3, 4, 128),
            scratch(2, 32, 128),
            scratch(7, 2, 32, 128),
            scratch(896, 128),
            scratch(896, 128),
            scratch(896, 128),
            scratch(192, 128),
            scratch(192, 128),
            scratch(192, 128),
            pltpu.SemaphoreType.DMA((N_COPIES,)),
            pltpu.SemaphoreType.DMA((N_COPIES,)),
            pltpu.SemaphoreType.DMA((6,)),
        ],
        compiler_params=pltpu.CompilerParams(
            collective_id=0, has_side_effects=True, vmem_limit_bytes=60 * 1024 * 1024
        ),
    )(
        velocity,
        input_weight.T,
        input_bias.reshape(1, 32),
        hidden_weight,
        hidden_bias.reshape(1, 32),
        output_weight.reshape(1, 32),
    )
    return pl.pallas_call(
        hand_over,
        out_shape=(
            jax.ShapeDtypeStruct((3, 16, 16, 128), F32),
            jax.ShapeDtypeStruct((16, 16, 128), F32),
        ),
        in_specs=[pl.BlockSpec(memory_space=pl.ANY)] * 2,
        out_specs=[pl.BlockSpec(memory_space=pl.ANY)] * 2,
        scratch_shapes=[pltpu.SemaphoreType.DMA((2,))],
        compiler_params=pltpu.CompilerParams(vmem_limit_bytes=1024 * 1024),
    )(*results)


def solution(mesh):
    return jax.shard_map(
        body,
        mesh=mesh,
        in_specs=(P(None, "gx", "gy", "gz"), P(), P(), P(), P(), P()),
        out_specs=(P(None, "gx", "gy", "gz"), P("gx", "gy", "gz")),
        check_vma=False,
    )
```
